32 devices in a mesh: sens: 4 (over x, core), par: 8 (over z, y).
Axes of the slice: x: 2, y: 2, z: 4, core: 2. Of those that a mesh axis runs over, the one named last changes fastest.
Arguments:
- model: bfloat16 [4, 128, 256], P('sens', 'par'), may hold values from -6 to 6
- kernel: bfloat16 [512, 128, 256], P('sens', 'par'), may hold values from -0.03125 to 0.03125
- observed: float32 [4, 512, 256], P(None, 'sens'), may hold values from -6 to 6
- weights: float32 [512], P('sens'), may hold values from 0.25 to 4
Outputs:
- gradient: float32 [4, 128, 256], P('sens', 'par')
- misfit: float32 [], replicated
The draws below stay inside these ranges and needn't reach their ends.
All inputs are finite; a program needn't handle non-finite values.
Results may differ from the reference program's by a relative error of at most 0.0027.
Values may be sent and summed in bfloat16 or wider, within the bound.
No kernel may reach another device: no remote copies, remote signals or barrier semaphores. Data moves between devices by JAX's collectives and lax.ppermute only.
A program may use at most 192 MiB of HBM per device.

```python
import math
import jax
import jax.numpy as jnp
from jax import lax

V = 4
S = 512
NT = 256
P_DEV = 16
PARAMETER_TOTAL = 128
N_PAR = 8


def block_scale(rng, dims, split, low, high):
    level, own = 1.0, jax.random.fold_in(rng, 6)
    for position, shards_of in split:
        draws = jnp.exp(jax.random.uniform(jax.random.fold_in(own, position), (shards_of,), jnp.float32, low / len(split), high / len(split)))
        level = level * jnp.repeat(draws, dims[position] // shards_of).reshape([-1 if axis == position else 1 for axis in range(len(dims))])
    return level


def scatter_about(own_key, extent, width, limit, pieces=(), kind=jnp.bfloat16):
    entries = jax.random.normal(own_key, extent, jnp.float32) * width
    if len(pieces) > 0:
        entries = block_scale(own_key, extent, pieces, -0.22, 0.18) * entries
    return jnp.clip(entries, min=-limit, max=limit).astype(kind)


def setup_inputs(seed: int = 0) -> dict:
    streams_of = jax.random.split(jax.random.key(seed), 5)
    return {
        "model": scatter_about(streams_of[0], (V, PARAMETER_TOTAL, NT), 1.0, 6.0, ((0, 4), (1, 8))),
        "kernel": scatter_about(streams_of[1], (S, PARAMETER_TOTAL, NT), (PARAMETER_TOTAL * NT) ** -0.5, 0.03125, ((0, 4), (1, 8))),
        "observed": scatter_about(streams_of[2], (V, S, NT), 0.7, 6.0, ((1, 4),), jnp.float32),
        "weights": jnp.clip(jnp.exp(math.log(4.0) - 2.7725887 * jax.random.uniform(streams_of[3], (S,), jnp.float32) ** block_scale(streams_of[3], (S,), ((0, 4),), -0.2, 0.2)), 0.25, 4.0),
    }


def causal_rows(series):
    length_steps = series.shape[-1]
    padded = jnp.concatenate([series, jnp.zeros_like(series)], axis=-1)
    reps = (1,) * (series.ndim - 1) + (length_steps,)
    flat = jnp.tile(padded, reps)
    stride = 2 * length_steps - 1
    flat = flat[..., : length_steps * stride].reshape(series.shape[:-1] + (length_steps, stride))
    return flat[..., :length_steps]


def leading_rows(series):
    length_steps = series.shape[-1]
    padded = jnp.concatenate([series, jnp.zeros_like(series)], axis=-1)
    reps = (1,) * (series.ndim - 1) + (length_steps + 1,)
    flat = jnp.tile(padded, reps)
    stride = 2 * length_steps + 1
    flat = flat[..., : length_steps * stride].reshape(series.shape[:-1] + (length_steps, stride))
    return flat[..., :length_steps]


def reference(model, kernel, observed, weights):
    slabs = kernel.reshape(S, N_PAR, P_DEV, NT).transpose(1, 0, 2, 3)
    model_slabs = model.reshape(V, N_PAR, P_DEV, NT)
    predicted_list = []
    for vector in range(V):
        def forward_step(carry, pair):
            kernel_slab, model_slab = pair
            toeplitz_operator = causal_rows(model_slab.astype(jnp.float32))
            term = jnp.einsum('spk,pkt->st', kernel_slab.astype(jnp.float32), toeplitz_operator)
            return carry + term, None
        summed, _ = lax.scan(forward_step, jnp.zeros((S, NT), jnp.float32), (slabs, model_slabs[vector]))
        predicted_list.append(summed)
    predicted = jnp.stack(predicted_list)
    mismatch = predicted - observed
    weighted_residual = weights[None, :, None] * mismatch
    misfit = 0.5 * jnp.sum(weighted_residual * mismatch) / (V * S * NT)
    residual = weighted_residual.astype(jnp.bfloat16)
    gradient_list = []
    for vector in range(V):
        shifted = leading_rows(residual[vector].astype(jnp.float32))

        def adjoint_slab(kernel_slab):
            return jnp.einsum('spk,skt->pt', kernel_slab.astype(jnp.float32), shifted)
        per_slab = lax.map(adjoint_slab, slabs)
        gradient_list.append(per_slab.reshape(PARAMETER_TOTAL, NT))
    gradient = jnp.stack(gradient_list)
    return gradient, misfit
```

```python
import functools

import jax
import jax.numpy as jnp
from jax import lax
from jax.experimental import pallas as pl
from jax.experimental.pallas import tpu as pltpu
from jax.sharding import PartitionSpec as P

EXTRA_ROWS = 16
MISFIT_ROWS = 8
VMEM_LIMIT = 24 * 1024 * 1024


def partners(size, step):
    return [(i, i ^ step) for i in range(size)]


def forward_body(vectors, lags, *refs):
    models, (x_ref, out_ref, ut_ref, u_ref, acc_ref) = refs[:vectors], refs[vectors:]
    steps, points, sensors = x_ref.shape
    lane = lax.broadcasted_iota(jnp.int32, (points, steps), 1)
    for v in range(vectors):
        series = models[v][0].astype(jnp.float32)
        for kl in range(lags):
            moved = series if kl == 0 else jnp.where(lane >= kl, pltpu.roll(series, kl, 1), 0.0)
            ut_ref[v, kl * points : (kl + 1) * points, :] = moved
        u_ref[v] = ut_ref[v].T.astype(jnp.bfloat16)
    for k0 in range(0, steps, 2 * lags):
        left = steps - k0
        pair = [x_ref[k : k + lags].reshape(lags * points, sensors) for k in (k0, k0 + lags)]
        rows = u_ref[:, :left, :].reshape(vectors * left, lags * points)
        term = jnp.dot(rows, jnp.concatenate(pair, axis=1), preferred_element_type=jnp.float32)
        term = term.reshape(vectors, left, 2 * sensors)
        if k0 == 0:
            acc_ref[...] = term[:, :, :sensors]
        else:
            acc_ref[:, k0:, :] += term[:, :, :sensors]
        acc_ref[:, k0 + lags :, :] += term[:, : left - lags, sensors:]
    out_ref[...] = acc_ref[...].astype(jnp.bfloat16)


def residual_body(terms_ref, observed_ref, weights_ref, out_ref):
    pieces, rows, sensors = terms_ref.shape
    predicted = terms_ref[0].astype(jnp.float32)
    for piece in range(1, pieces):
        predicted += terms_ref[piece].astype(jnp.float32)
    mismatch = predicted - observed_ref[...]
    weighted = weights_ref[...] * mismatch
    out_ref[:rows, :] = weighted.astype(jnp.bfloat16)
    squared = jnp.sum(weighted * mismatch, axis=0, keepdims=True)
    high = squared.astype(jnp.bfloat16).astype(jnp.float32)
    rest = squared - high
    middle = rest.astype(jnp.bfloat16).astype(jnp.float32)
    low = rest - middle
    row = lax.broadcasted_iota(jnp.int32, (EXTRA_ROWS, sensors), 0)
    parts = jnp.where(row == 0, high, jnp.where(row == 1, middle, jnp.where(row == 2, low, 0.0)))
    out_ref[rows:, :] = parts.astype(jnp.bfloat16)


def adjoint_body(vectors, lags, gathered_ref, x_ref, *refs):
    outs, (a_ref, r_ref) = refs[:vectors], refs[vectors:]
    steps, points, sensors = x_ref.shape
    pieces, rows = gathered_ref.shape[0], gathered_ref.shape[1] - EXTRA_ROWS
    blocks = steps // lags
    per_vector = steps // rows
    for d in range(lags):
        for c in range(blocks):
            a_ref[c * points : (c + 1) * points, d * sensors : (d + 1) * sensors] = x_ref[c * lags + d]
    extra = gathered_ref[0, rows:, :].astype(jnp.float32)
    for piece in range(1, pieces):
        extra += gathered_ref[piece, rows:, :].astype(jnp.float32)
    squared = jnp.sum(extra)
    lane = lax.broadcasted_iota(jnp.int32, (sensors, steps), 1)
    lane_p = lax.broadcasted_iota(jnp.int32, (points, steps), 1)
    for v in range(vectors):
        chunks = [gathered_ref[v * per_vector + i, :rows, :].astype(jnp.float32) for i in range(per_vector)]
        series = jnp.concatenate(chunks, axis=0).T
        for d in range(lags):
            moved = series
            if d > 0:
                moved = jnp.where(lane < steps - d, pltpu.roll(series, steps - d, 1), 0.0)
            r_ref[v, d * sensors : (d + 1) * sensors, :] = moved.astype(jnp.bfloat16)
        terms = jnp.dot(a_ref[...], r_ref[v], preferred_element_type=jnp.float32)
        total = terms[:points]
        for c in range(1, blocks):
            moved = pltpu.roll(terms[c * points : (c + 1) * points], steps - c * lags, 1)
            total += jnp.where(lane_p < steps - c * lags, moved, 0.0)
        outs[v][:points, :] = total
        outs[v][points:, :] = jnp.full((MISFIT_ROWS, steps), squared, jnp.float32)


def local(model, kernel, observed, weights):
    n_sens, n_par = lax.axis_size("sens"), lax.axis_size("par")
    me, j = lax.axis_index("sens"), lax.axis_index("par")
    sensors, points, steps = kernel.shape
    vectors = n_sens * model.shape[0]
    lags = 256 // points
    rows = vectors * steps // n_par
    vmem = pl.BlockSpec(memory_space=pltpu.VMEM)
    params = pltpu.CompilerParams(vmem_limit_bytes=VMEM_LIMIT)
    flops = 2 * vectors * sensors * points * steps * steps

    models = [model] + [lax.ppermute(model, "sens", partners(n_sens, step)) for step in range(1, n_sens)]
    x = jnp.transpose(kernel, (2, 1, 0))
    first = j * rows
    source = me ^ (first // steps)
    own = lax.dynamic_slice(observed, (source, 0, first % steps), (1, sensors, rows))
    own = own[0].T

    terms = pl.pallas_call(
        functools.partial(forward_body, vectors, lags),
        out_shape=jax.ShapeDtypeStruct((vectors, steps, sensors), jnp.bfloat16),
        in_specs=[vmem] * (vectors + 1),
        out_specs=vmem,
        scratch_shapes=[
            pltpu.VMEM((vectors, lags * points, steps), jnp.float32),
            pltpu.VMEM((vectors, steps, lags * points), jnp.bfloat16),
            pltpu.VMEM((vectors, steps, sensors), jnp.float32),
        ],
        compiler_params=params,
        cost_estimate=pl.CostEstimate(flops=flops, bytes_accessed=2 * kernel.size, transcendentals=0),
    )(*models, x)

    pieces = lax.all_to_all(terms.reshape(n_par, rows, sensors), "par", 0, 0)
    own_residual = pl.pallas_call(
        residual_body,
        out_shape=jax.ShapeDtypeStruct((rows + EXTRA_ROWS, sensors), jnp.bfloat16),
        in_specs=[vmem] * 3,
        out_specs=vmem,
        compiler_params=params,
    )(pieces, own, weights[None, :])
    gathered = lax.all_gather(own_residual, "par", axis=0)

    partials = pl.pallas_call(
        functools.partial(adjoint_body, vectors, lags),
        out_shape=[jax.ShapeDtypeStruct((points + MISFIT_ROWS, steps), jnp.float32)] * vectors,
        in_specs=[vmem] * 2,
        out_specs=[vmem] * vectors,
        scratch_shapes=[
            pltpu.VMEM((steps // lags * points, lags * sensors), jnp.bfloat16),
            pltpu.VMEM((vectors, lags * sensors, steps), jnp.bfloat16),
        ],
        compiler_params=params,
        cost_estimate=pl.CostEstimate(flops=flops, bytes_accessed=2 * kernel.size, transcendentals=0),
    )(gathered, x)
    total = partials[0]
    for step in range(1, n_sens):
        total += lax.ppermute(partials[step], "sens", partners(n_sens, step))
    entries = vectors * sensors * n_sens * steps
    misfit = total[points, 0] * (0.5 / entries)
    return (total[None, :points, :], misfit)


def solution(mesh):
    return jax.shard_map(
        local,
        mesh=mesh,
        in_specs=(P("sens", "par", None), P("sens", "par", None), P(None, "sens", None), P("sens")),
        out_specs=(P("sens", "par", None), P()),
        check_vma=False,
    )
```

```python
import functools

import jax
import jax.numpy as jnp
from jax import lax
from jax.experimental import pallas as pl
from jax.experimental.pallas import tpu as pltpu
from jax.sharding import PartitionSpec as P

EXTRA_ROWS = 16
WEIGHT_ROWS = 8
MISFIT_ROWS = 8
VMEM_LIMIT = 24 * 1024 * 1024


def swap(value, axis, step):
    return lax.ppermute(value, axis, [(i, i ^ step) for i in range(lax.axis_size(axis))])


def forward_body(vectors, pieces, lags, *refs):
    models, refs = refs[:vectors], refs[vectors:]
    x_ref, observed_ref, weights_ref, own_ref = refs[:4]
    sent, refs = refs[4 : 3 + pieces], refs[3 + pieces :]
    ut_ref, u_ref, acc_ref, seen_ref, scale_ref, sems = refs
    steps, points, sensors = x_ref.shape
    rows = vectors * steps // pieces
    me, j = lax.axis_index("sens"), lax.axis_index("par")
    first = j * rows
    fetch_seen = pltpu.make_async_copy(observed_ref.at[me ^ (first // steps)], seen_ref, sems.at[0])
    fetch_scale = pltpu.make_async_copy(weights_ref, scale_ref, sems.at[1])
    fetch_seen.start()
    fetch_scale.start()
    lane = lax.broadcasted_iota(jnp.int32, (points, steps), 1)
    for v in range(vectors):
        series = models[v][0].astype(jnp.float32)
        for kl in range(lags):
            moved = series if kl == 0 else jnp.where(lane >= kl, pltpu.roll(series, kl, 1), 0.0)
            ut_ref[v, kl * points : (kl + 1) * points, :] = moved
        u_ref[v] = ut_ref[v].T.astype(jnp.bfloat16)
    for k0 in range(0, steps, 2 * lags):
        left = steps - k0
        pair = [x_ref[k : k + lags].reshape(lags * points, sensors) for k in (k0, k0 + lags)]
        some = u_ref[:, :left, :].reshape(vectors * left, lags * points)
        term = jnp.dot(some, jnp.concatenate(pair, axis=1), preferred_element_type=jnp.float32)
        for v in range(vectors):
            at, end = v * steps, (v + 1) * steps
            part = term[v * left : (v + 1) * left]
            if k0 == 0:
                acc_ref[at:end, :] = part[:, :sensors]
            else:
                acc_ref[at + k0 : end, :] += part[:, :sensors]
            acc_ref[at + k0 + lags : end, :] += part[: left - lags, sensors:]
    for step in range(1, pieces):
        there = pl.multiple_of((j ^ step) * rows, rows)
        sent[step - 1][...] = acc_ref[pl.ds(there, rows), :].astype(jnp.bfloat16)
    fetch_seen.wait()
    fetch_scale.wait()
    ut_ref[0, :, :sensors] = seen_ref[...].T
    here = pl.multiple_of(first, rows)
    seen = ut_ref[0, pl.ds(pl.multiple_of(first % steps, rows), rows), :sensors]
    own_ref[:rows, :] = acc_ref[pl.ds(here, rows), :] - seen
    own_ref[rows:, :] = jnp.broadcast_to(scale_ref[...], (WEIGHT_ROWS, sensors))


def residual_body(own_ref, *refs):
    terms, out_ref = refs[:-1], refs[-1]
    rows, sensors = terms[0].shape
    mismatch = own_ref[:rows, :]
    for term in terms:
        mismatch += term[...].astype(jnp.float32)
    weighted = own_ref[rows : rows + 1, :] * mismatch
    out_ref[:rows, :] = weighted.astype(jnp.bfloat16)
    squared = jnp.sum(weighted * mismatch, axis=0, keepdims=True)
    high = squared.astype(jnp.bfloat16).astype(jnp.float32)
    rest = squared - high
    middle = rest.astype(jnp.bfloat16).astype(jnp.float32)
    low = rest - middle
    row = lax.broadcasted_iota(jnp.int32, (EXTRA_ROWS, sensors), 0)
    parts = jnp.where(row == 0, high, jnp.where(row == 1, middle, jnp.where(row == 2, low, 0.0)))
    out_ref[rows:, :] = parts.astype(jnp.bfloat16)


def adjoint_body(vectors, pieces, lags, *refs):
    gathered, x_ref = refs[:pieces], refs[pieces]
    outs, (a_ref, r_ref, all_ref) = refs[pieces + 1 : pieces + 1 + vectors], refs[pieces + 1 + vectors :]
    steps, points, sensors = x_ref.shape
    rows = vectors * steps // pieces
    blocks = steps // lags
    j = lax.axis_index("par")
    for d in range(lags):
        for c in range(blocks):
            a_ref[c * points : (c + 1) * points, d * sensors : (d + 1) * sensors] = x_ref[c * lags + d]
    extra = jnp.zeros((EXTRA_ROWS, sensors), jnp.float32)
    for step in range(pieces):
        there = pl.multiple_of((j ^ step) * rows, rows)
        all_ref[pl.ds(there, rows), :] = gathered[step][:rows, :].astype(jnp.float32)
        extra += gathered[step][rows:, :].astype(jnp.float32)
    squared = jnp.sum(extra)
    lane = lax.broadcasted_iota(jnp.int32, (sensors, steps), 1)
    lane_p = lax.broadcasted_iota(jnp.int32, (points, steps), 1)
    for v in range(vectors):
        series = all_ref[v * steps : (v + 1) * steps, :].T
        for d in range(lags):
            moved = series
            if d > 0:
                moved = jnp.where(lane < steps - d, pltpu.roll(series, steps - d, 1), 0.0)
            r_ref[v, d * sensors : (d + 1) * sensors, :] = moved.astype(jnp.bfloat16)
        terms = jnp.dot(a_ref[...], r_ref[v], preferred_element_type=jnp.float32)
        total = terms[:points]
        for c in range(1, blocks):
            moved = pltpu.roll(terms[c * points : (c + 1) * points], steps - c * lags, 1)
            total += jnp.where(lane_p < steps - c * lags, moved, 0.0)
        outs[v][:points, :] = total
        outs[v][points:, :] = jnp.full((MISFIT_ROWS, steps), squared, jnp.float32)


def total_body(scale, *refs):
    terms, (gradient_ref, misfit_ref) = refs[:-2], refs[-2:]
    points = gradient_ref.shape[1]
    total = terms[0][...]
    for term in terms[1:]:
        total += term[...]
    gradient_ref[0] = total[:points]
    misfit_ref[...] = total[points : points + 1, :1] * scale


def local(model, kernel, observed, weights):
    n_sens, n_par = lax.axis_size("sens"), lax.axis_size("par")
    sensors, points, steps = kernel.shape
    vectors = n_sens * model.shape[0]
    lags = 256 // points
    rows = vectors * steps // n_par
    vmem = pl.BlockSpec(memory_space=pltpu.VMEM)
    anywhere = pl.BlockSpec(memory_space=pl.ANY)
    params = pltpu.CompilerParams(vmem_limit_bytes=VMEM_LIMIT)
    flops = 2 * vectors * sensors * points * steps * steps
    cost = pl.CostEstimate(flops=flops, bytes_accessed=2 * kernel.size, transcendentals=0)

    models = [model] + [swap(model, "sens", step) for step in range(1, n_sens)]
    x = jnp.transpose(kernel, (2, 1, 0))

    piece = jax.ShapeDtypeStruct((rows, sensors), jnp.bfloat16)
    own, *sent = pl.pallas_call(
        functools.partial(forward_body, vectors, n_par, lags),
        out_shape=[jax.ShapeDtypeStruct((rows + WEIGHT_ROWS, sensors), jnp.float32)] + [piece] * (n_par - 1),
        in_specs=[vmem] * (vectors + 1) + [anywhere] * 2,
        out_specs=[vmem] * n_par,
        scratch_shapes=[
            pltpu.VMEM((vectors, lags * points, steps), jnp.float32),
            pltpu.VMEM((vectors, steps, lags * points), jnp.bfloat16),
            pltpu.VMEM((vectors * steps, sensors), jnp.float32),
            pltpu.VMEM((sensors, steps), jnp.float32),
            pltpu.VMEM((1, sensors), jnp.float32),
            pltpu.SemaphoreType.DMA((2,)),
        ],
        compiler_params=params,
        cost_estimate=cost,
    )(*models, x, observed, weights[None, :])

    terms = [swap(sent[step - 1], "par", step) for step in range(n_par - 1, 0, -1)]
    residual = pl.pallas_call(
        residual_body,
        out_shape=jax.ShapeDtypeStruct((rows + EXTRA_ROWS, sensors), jnp.bfloat16),
        in_specs=[vmem] * n_par,
        out_specs=vmem,
        compiler_params=params,
    )(own, *terms)
    gathered = [swap(residual, "par", step) for step in range(n_par - 1, 0, -1)]

    partials = pl.pallas_call(
        functools.partial(adjoint_body, vectors, n_par, lags),
        out_shape=[jax.ShapeDtypeStruct((points + MISFIT_ROWS, steps), jnp.float32)] * vectors,
        in_specs=[vmem] * (n_par + 1),
        out_specs=[vmem] * vectors,
        scratch_shapes=[
            pltpu.VMEM((steps // lags * points, lags * sensors), jnp.bfloat16),
            pltpu.VMEM((vectors, lags * sensors, steps), jnp.bfloat16),
            pltpu.VMEM((vectors * steps, sensors), jnp.float32),
        ],
        compiler_params=params,
        cost_estimate=cost,
    )(residual, *gathered[::-1], x)

    received = [swap(partials[step], "sens", step) for step in range(n_sens - 1, 0, -1)]
    entries = vectors * sensors * n_sens * steps
    gradient, misfit = pl.pallas_call(
        functools.partial(total_body, 0.5 / entries),
        out_shape=[
            jax.ShapeDtypeStruct((1, points, steps), jnp.float32),
            jax.ShapeDtypeStruct((1, 1), jnp.float32),
        ],
        in_specs=[vmem] * n_sens,
        out_specs=[vmem] * 2,
    )(partials[0], *received)
    return (gradient, misfit[0, 0])


def solution(mesh):
    return jax.shard_map(
        local,
        mesh=mesh,
        in_specs=(P("sens", "par", None), P("sens", "par", None), P(None, "sens", None), P("sens")),
        out_specs=(P("sens", "par", None), P()),
        check_vma=False,
    )
```

```python
import functools

import jax
import jax.numpy as jnp
from jax import lax
from jax.experimental import pallas as pl
from jax.experimental.pallas import tpu as pltpu
from jax.sharding import PartitionSpec as P

EXTRA_ROWS = 16
WEIGHT_ROWS = 8
MISFIT_ROWS = 8
VMEM_LIMIT = 24 * 1024 * 1024
SMALL_LIMIT = 4 * 1024 * 1024


def swap(value, axis, step):
    return lax.ppermute(value, axis, [(i, i ^ step) for i in range(lax.axis_size(axis))])


def levels(size):
    near = 1
    while near * near * 4 <= size:
        near *= 2
    return near, size // near


def forward_body(vectors, near, far, lags, *refs):
    models, refs = refs[:vectors], refs[vectors:]
    x_ref, observed_ref, weights_ref, own_ref = refs[:4]
    sent, refs = refs[4 : 3 + near], refs[3 + near :]
    ut_ref, u_ref, acc_ref, seen_ref, scale_ref, sems = refs
    steps, points, sensors = x_ref.shape
    rows = vectors * steps // (near * far)
    me, j = lax.axis_index("sens"), lax.axis_index("par")
    first = j * rows
    fetch_seen = pltpu.make_async_copy(observed_ref.at[me ^ (first // steps)], seen_ref, sems.at[0])
    fetch_scale = pltpu.make_async_copy(weights_ref, scale_ref, sems.at[1])
    fetch_seen.start()
    fetch_scale.start()
    lane = lax.broadcasted_iota(jnp.int32, (points, steps), 1)
    for v in range(vectors):
        series = models[v][0].astype(jnp.float32)
        for kl in range(lags):
            moved = series if kl == 0 else jnp.where(lane >= kl, pltpu.roll(series, kl, 1), 0.0)
            ut_ref[v, kl * points : (kl + 1) * points, :] = moved
        u_ref[v] = ut_ref[v].T.astype(jnp.bfloat16)
    for k0 in range(0, steps, 2 * lags):
        left = steps - k0
        pair = [x_ref[k : k + lags].reshape(lags * points, sensors) for k in (k0, k0 + lags)]
        some = u_ref[:, :left, :].reshape(vectors * left, lags * points)
        term = jnp.dot(some, jnp.concatenate(pair, axis=1), preferred_element_type=jnp.float32)
        for v in range(vectors):
            at, end = v * steps, (v + 1) * steps
            part = term[v * left : (v + 1) * left]
            if k0 == 0:
                acc_ref[at:end, :] = part[:, :sensors]
            else:
                acc_ref[at + k0 : end, :] += part[:, :sensors]
            acc_ref[at + k0 + lags : end, :] += part[: left - lags, sensors:]
    for b in range(far):
        for a in range(near):
            there = pl.multiple_of((j ^ (b * near + a)) * rows, rows)
            part = acc_ref[pl.ds(there, rows), :]
            if a == 0:
                own_ref[b * rows : (b + 1) * rows, :] = part
            else:
                sent[a - 1][b * rows : (b + 1) * rows, :] = part.astype(jnp.bfloat16)
    fetch_seen.wait()
    fetch_scale.wait()
    ut_ref[0, :, :sensors] = seen_ref[...].T
    own_ref[:rows, :] -= ut_ref[0, pl.ds(pl.multiple_of(first % steps, rows), rows), :sensors]
    own_ref[far * rows :, :] = jnp.broadcast_to(scale_ref[...], (WEIGHT_ROWS, sensors))


def middle_body(near, far, own_ref, *refs):
    terms, out_ref, sent = refs[: near - 1], refs[near - 1], refs[near:]
    rows = (own_ref.shape[0] - WEIGHT_ROWS) // far
    for b in range(far):
        part = own_ref[b * rows : (b + 1) * rows, :]
        for term in terms:
            part += term[b * rows : (b + 1) * rows, :].astype(jnp.float32)
        if b == 0:
            out_ref[:rows, :] = part
        else:
            sent[b - 1][...] = part.astype(jnp.bfloat16)
    out_ref[rows:, :] = own_ref[far * rows :, :]


def residual_body(own_ref, *refs):
    terms, out_ref = refs[:-1], refs[-1]
    rows, sensors = terms[0].shape
    mismatch = own_ref[:rows, :]
    for term in terms:
        mismatch += term[...].astype(jnp.float32)
    weighted = own_ref[rows : rows + 1, :] * mismatch
    out_ref[:rows, :] = weighted.astype(jnp.bfloat16)
    squared = jnp.sum(weighted * mismatch, axis=0, keepdims=True)
    high = squared.astype(jnp.bfloat16).astype(jnp.float32)
    rest = squared - high
    middle = rest.astype(jnp.bfloat16).astype(jnp.float32)
    low = rest - middle
    row = lax.broadcasted_iota(jnp.int32, (EXTRA_ROWS, sensors), 0)
    parts = jnp.where(row == 0, high, jnp.where(row == 1, middle, jnp.where(row == 2, low, 0.0)))
    out_ref[rows:, :] = parts.astype(jnp.bfloat16)


def join_body(*refs):
    parts, out_ref = refs[:-1], refs[-1]
    rows = parts[0].shape[0]
    for b, part in enumerate(parts):
        out_ref[b * rows : (b + 1) * rows, :] = part[...]


def adjoint_body(vectors, near, far, lags, *refs):
    gathered, x_ref = refs[:near], refs[near]
    outs, (a_ref, r_ref, all_ref) = refs[near + 1 : near + 1 + vectors], refs[near + 1 + vectors :]
    steps, points, sensors = x_ref.shape
    rows = vectors * steps // (near * far)
    blocks = steps // lags
    j = lax.axis_index("par")
    for d in range(lags):
        for c in range(blocks):
            a_ref[c * points : (c + 1) * points, d * sensors : (d + 1) * sensors] = x_ref[c * lags + d]
    extra = jnp.zeros((EXTRA_ROWS, sensors), jnp.float32)
    for b in range(far):
        for a in range(near):
            there = pl.multiple_of((j ^ (b * near + a)) * rows, rows)
            at = b * (rows + EXTRA_ROWS)
            all_ref[pl.ds(there, rows), :] = gathered[a][at : at + rows, :].astype(jnp.float32)
            extra += gathered[a][at + rows : at + rows + EXTRA_ROWS, :].astype(jnp.float32)
    squared = jnp.sum(extra)
    lane = lax.broadcasted_iota(jnp.int32, (sensors, steps), 1)
    lane_p = lax.broadcasted_iota(jnp.int32, (points, steps), 1)
    for v in range(vectors):
        series = all_ref[v * steps : (v + 1) * steps, :].T
        for d in range(lags):
            moved = series
            if d > 0:
                moved = jnp.where(lane < steps - d, pltpu.roll(series, steps - d, 1), 0.0)
            r_ref[v, d * sensors : (d + 1) * sensors, :] = moved.astype(jnp.bfloat16)
        terms = jnp.dot(a_ref[...], r_ref[v], preferred_element_type=jnp.float32)
        total = terms[:points]
        for c in range(1, blocks):
            moved = pltpu.roll(terms[c * points : (c + 1) * points], steps - c * lags, 1)
            total += jnp.where(lane_p < steps - c * lags, moved, 0.0)
        outs[v][:points, :] = total
        outs[v][points:, :] = jnp.full((MISFIT_ROWS, steps), squared, jnp.float32)


def total_body(scale, *refs):
    terms, (gradient_ref, misfit_ref) = refs[:-2], refs[-2:]
    points = gradient_ref.shape[1]
    total = terms[0][...]
    for term in terms[1:]:
        total += term[...]
    gradient_ref[0] = total[:points]
    misfit_ref[...] = total[points : points + 1, :1] * scale


def call(body, out_shape, operands, limit=SMALL_LIMIT, **options):
    vmem = pl.BlockSpec(memory_space=pltpu.VMEM)
    options.setdefault("in_specs", [vmem] * len(operands))
    return pl.pallas_call(
        body,
        out_shape=out_shape,
        out_specs=jax.tree.map(lambda _: vmem, out_shape),
        compiler_params=pltpu.CompilerParams(vmem_limit_bytes=limit),
        **options,
    )(*operands)


def local(model, kernel, observed, weights):
    n_sens, n_par = lax.axis_size("sens"), lax.axis_size("par")
    near, far = levels(n_par)
    sensors, points, steps = kernel.shape
    vectors = n_sens * model.shape[0]
    lags = 256 // points
    rows = vectors * steps // n_par
    flops = 2 * vectors * sensors * points * steps * steps
    cost = pl.CostEstimate(flops=flops, bytes_accessed=2 * kernel.size, transcendentals=0)

    models = [model] + [swap(model, "sens", step) for step in range(1, n_sens)]
    x = jnp.transpose(kernel, (2, 1, 0))

    vmem, hbm = pl.BlockSpec(memory_space=pltpu.VMEM), pl.BlockSpec(memory_space=pltpu.HBM)
    own, *sent = call(
        functools.partial(forward_body, vectors, near, far, lags),
        [jax.ShapeDtypeStruct((far * rows + WEIGHT_ROWS, sensors), jnp.float32)]
        + [jax.ShapeDtypeStruct((far * rows, sensors), jnp.bfloat16)] * (near - 1),
        (*models, x, observed, weights[None, :]),
        VMEM_LIMIT,
        in_specs=[vmem] * (vectors + 1) + [hbm] * 2,
        scratch_shapes=[
            pltpu.VMEM((vectors, lags * points, steps), jnp.float32),
            pltpu.VMEM((vectors, steps, lags * points), jnp.bfloat16),
            pltpu.VMEM((vectors * steps, sensors), jnp.float32),
            pltpu.VMEM((sensors, steps), jnp.float32),
            pltpu.VMEM((1, sensors), jnp.float32),
            pltpu.SemaphoreType.DMA((2,)),
        ],
        cost_estimate=cost,
    )

    terms = [swap(sent[a - 1], "par", a) for a in range(1, near)]
    own, *sent = call(
        functools.partial(middle_body, near, far),
        [jax.ShapeDtypeStruct((rows + WEIGHT_ROWS, sensors), jnp.float32)]
        + [jax.ShapeDtypeStruct((rows, sensors), jnp.bfloat16)] * (far - 1),
        (own, *terms),
    )
    terms = [swap(sent[b - 1], "par", b * near) for b in range(far - 1, 0, -1)]
    residual = call(
        residual_body,
        jax.ShapeDtypeStruct((rows + EXTRA_ROWS, sensors), jnp.bfloat16),
        (own, *terms),
    )
    parts = [swap(residual, "par", b * near) for b in range(far - 1, 0, -1)]
    block = call(
        join_body,
        jax.ShapeDtypeStruct((far * (rows + EXTRA_ROWS), sensors), jnp.bfloat16),
        (residual, *parts[::-1]),
    )
    gathered = [block] + [swap(block, "par", a) for a in range(1, near)]

    partials = call(
        functools.partial(adjoint_body, vectors, near, far, lags),
        [jax.ShapeDtypeStruct((points + MISFIT_ROWS, steps), jnp.float32)] * vectors,
        (*gathered, x),
        VMEM_LIMIT,
        scratch_shapes=[
            pltpu.VMEM((steps // lags * points, lags * sensors), jnp.bfloat16),
            pltpu.VMEM((vectors, lags * sensors, steps), jnp.bfloat16),
            pltpu.VMEM((vectors * steps, sensors), jnp.float32),
        ],
        cost_estimate=cost,
    )

    received = [swap(partials[step], "sens", step) for step in range(n_sens - 1, 0, -1)]
    entries = vectors * sensors * n_sens * steps
    gradient, misfit = call(
        functools.partial(total_body, 0.5 / entries),
        [jax.ShapeDtypeStruct((1, points, steps), jnp.float32), jax.ShapeDtypeStruct((1, 1), jnp.float32)],
        (partials[0], *received),
    )
    return (gradient, misfit[0, 0])


def solution(mesh):
    return jax.shard_map(
        local,
        mesh=mesh,
        in_specs=(P("sens", "par", None), P("sens", "par", None), P(None, "sens", None), P("sens")),
        out_specs=(P("sens", "par", None), P()),
        check_vma=False,
    )
```

```python
import functools

import jax
import jax.numpy as jnp
from jax import lax
from jax.experimental import pallas as pl
from jax.experimental.pallas import tpu as pltpu
from jax.sharding import PartitionSpec as P

EXTRA_ROWS = 16
WEIGHT_ROWS = 8
MISFIT_ROWS = 8
VMEM_LIMIT = 24 * 1024 * 1024
SMALL_LIMIT = 4 * 1024 * 1024


def swap(value, axis, step):
    return lax.ppermute(value, axis, [(i, i ^ step) for i in range(lax.axis_size(axis))])


def levels(size, vectors):
    near = 1
    while near * near * 4 <= size and near * 2 <= vectors:
        near *= 2
    return near, size // near


def turn_body(start, kernel_ref, out_ref, rows_ref, turned_ref):
    count, points, sensors = out_ref.shape
    rows_ref[...] = kernel_ref[:, :, start : start + count].astype(jnp.float32).reshape(sensors * points, count)
    for p in range(points):
        plane = rows_ref[pl.ds(p, sensors, stride=points), :]
        turned_ref[pl.ds(p, count, stride=points), :] = plane.T
    out_ref[...] = turned_ref[...].reshape(count, points, sensors).astype(jnp.bfloat16)


def forward_body(away, near, far, lags, n_models, n_x, *refs):
    models, xs, refs = refs[:n_models], refs[n_models : n_models + n_x], refs[n_models + n_x :]
    part_steps, points, sensors = xs[0].shape
    steps = part_steps * n_x
    me, j = lax.axis_index("sens"), lax.axis_index("par")
    place, block = j // near, lax.rem(j, near) ^ away
    if away == 0:
        observed_ref, weights_ref, out_ref, all_ref, ut_ref, u_ref, acc_ref, seen_ref, scale_ref, sems = refs
    else:
        out_ref, all_ref, ut_ref, u_ref, acc_ref = refs
    vectors, of_block = all_ref.shape[0], u_ref.shape[0]
    rows = of_block * steps // far
    if away == 0:
        first = (block * far + place) * rows
        fetch_seen = pltpu.make_async_copy(observed_ref.at[me ^ (first // steps)], seen_ref, sems.at[0])
        fetch_scale = pltpu.make_async_copy(weights_ref, scale_ref, sems.at[1])
        fetch_seen.start()
        fetch_scale.start()
    lane = lax.broadcasted_iota(jnp.int32, (points, steps), 1)
    for v in range(vectors):
        ref = models[v * n_models // vectors]
        all_ref[v] = ref[v % ref.shape[0]].astype(jnp.float32)
    for v in range(of_block):
        series = all_ref[block * of_block + v]
        for kl in range(lags):
            moved = series if kl == 0 else jnp.where(lane >= kl, pltpu.roll(series, kl, 1), 0.0)
            ut_ref[v, kl * points : (kl + 1) * points, :] = moved
        u_ref[v] = ut_ref[v].T.astype(jnp.bfloat16)
    for k0 in range(0, steps, 2 * lags):
        left = steps - k0
        x_ref, at = xs[k0 // part_steps], k0 % part_steps
        pair = [x_ref[k : k + lags].reshape(lags * points, sensors) for k in (at, at + lags)]
        some = u_ref[:, :left, :].reshape(of_block * left, lags * points)
        term = jnp.dot(some, jnp.concatenate(pair, axis=1), preferred_element_type=jnp.float32)
        for v in range(of_block):
            at, end = v * steps, (v + 1) * steps
            part = term[v * left : (v + 1) * left]
            if k0 == 0:
                acc_ref[at:end, :] = part[:, :sensors]
            else:
                acc_ref[at + k0 : end, :] += part[:, :sensors]
            acc_ref[at + k0 + lags : end, :] += part[: left - lags, sensors:]
    for b in range(far):
        there = pl.multiple_of((place ^ b) * rows, rows)
        out_ref[b * rows : (b + 1) * rows, :] = acc_ref[pl.ds(there, rows), :].astype(out_ref.dtype)
    if away == 0:
        fetch_seen.wait()
        fetch_scale.wait()
        ut_ref[0, :, :sensors] = seen_ref[...].T
        out_ref[:rows, :] -= ut_ref[0, pl.ds(pl.multiple_of(first % steps, rows), rows), :sensors]
        out_ref[far * rows :, :] = jnp.broadcast_to(scale_ref[...], (WEIGHT_ROWS, sensors))


def middle_body(near, far, own_ref, *refs):
    terms, out_ref, sent = refs[: near - 1], refs[near - 1], refs[near:]
    rows = (own_ref.shape[0] - WEIGHT_ROWS) // far
    for b in range(far):
        part = own_ref[b * rows : (b + 1) * rows, :]
        for term in terms:
            part += term[b * rows : (b + 1) * rows, :].astype(jnp.float32)
        if b == 0:
            out_ref[:rows, :] = part
        else:
            sent[b - 1][...] = part.astype(jnp.bfloat16)
    out_ref[rows:, :] = own_ref[far * rows :, :]


def residual_body(own_ref, *refs):
    terms, out_ref = refs[:-1], refs[-1]
    rows, sensors = terms[0].shape
    mismatch = own_ref[:rows, :]
    for term in terms:
        mismatch += term[...].astype(jnp.float32)
    weighted = own_ref[rows : rows + 1, :] * mismatch
    out_ref[:rows, :] = weighted.astype(jnp.bfloat16)
    squared = jnp.sum(weighted * mismatch, axis=0, keepdims=True)
    high = squared.astype(jnp.bfloat16).astype(jnp.float32)
    rest = squared - high
    middle = rest.astype(jnp.bfloat16).astype(jnp.float32)
    low = rest - middle
    row = lax.broadcasted_iota(jnp.int32, (EXTRA_ROWS, sensors), 0)
    parts = jnp.where(row == 0, high, jnp.where(row == 1, middle, jnp.where(row == 2, low, 0.0)))
    out_ref[rows:, :] = parts.astype(jnp.bfloat16)


def join_body(*refs):
    parts, out_ref = refs[:-1], refs[-1]
    rows = parts[0].shape[0]
    for b, part in enumerate(parts):
        out_ref[b * rows : (b + 1) * rows] = part[...]


def adjoint_terms(block_ref, left_ref, r_ref, all_ref, far, lags, points):
    of_block, _, steps = r_ref.shape
    sensors = all_ref.shape[1]
    rows = of_block * steps // far
    place = lax.axis_index("par") // (lax.axis_size("par") // far)
    for b in range(far):
        there = pl.multiple_of((place ^ b) * rows, rows)
        at = b * (rows + EXTRA_ROWS)
        all_ref[pl.ds(there, rows), :] = block_ref[at : at + rows, :].astype(jnp.float32)
    lane = lax.broadcasted_iota(jnp.int32, (sensors, steps), 1)
    lane_p = lax.broadcasted_iota(jnp.int32, (points, steps), 1)
    for v in range(of_block):
        series = all_ref[v * steps : (v + 1) * steps, :].T
        for d in range(lags):
            moved = series
            if d > 0:
                moved = jnp.where(lane < steps - d, pltpu.roll(series, steps - d, 1), 0.0)
            r_ref[v, d * sensors : (d + 1) * sensors, :] = moved.astype(jnp.bfloat16)
        terms = jnp.dot(left_ref[...], r_ref[v], preferred_element_type=jnp.float32)
        total = terms[:points]
        for c in range(1, steps // lags):
            moved = pltpu.roll(terms[c * points : (c + 1) * points], steps - c * lags, 1)
            total += jnp.where(lane_p < steps - c * lags, moved, 0.0)
        yield v, total


def adjoint_own_body(far, lags, block_ref, *refs):
    xs, (left_ref, own_ref, r_ref, all_ref) = refs[:-4], refs[-4:]
    part_steps, points, sensors = xs[0].shape
    for d in range(lags):
        for c in range(len(xs) * part_steps // lags):
            k = c * lags + d
            left_ref[c * points : (c + 1) * points, d * sensors : (d + 1) * sensors] = xs[k // part_steps][k % part_steps]
    for v, total in adjoint_terms(block_ref, left_ref, r_ref, all_ref, far, lags, points):
        own_ref[v] = total


def adjoint_rest_body(far, lags, own_ref, left_ref, own_block_ref, *refs):
    blocks, (kept_ref, sent_ref, slots_ref, r_ref, all_ref) = refs[:-5], refs[-5:]
    of_block, points, steps = own_ref.shape
    near = len(blocks) + 1
    rows = of_block * steps // far
    block = lax.rem(lax.axis_index("par"), near)
    extra = 0.0
    for ref in (own_block_ref, *blocks):
        for b in range(far):
            at = b * (rows + EXTRA_ROWS) + rows
            extra += ref[at : at + EXTRA_ROWS, :].astype(jnp.float32)
    squared = jnp.full((MISFIT_ROWS, steps), jnp.sum(extra), jnp.float32)
    for v in range(of_block):
        slots_ref[block * of_block + v] = own_ref[v]
    for away, ref in enumerate(blocks, 1):
        for v, total in adjoint_terms(ref, left_ref, r_ref, all_ref, far, lags, points):
            slots_ref[(block ^ away) * of_block + v] = total
    for half, ref in enumerate((kept_ref, sent_ref)):
        for i in range(ref.shape[0]):
            ref[i, :points, :] = slots_ref[2 * i + half]
            ref[i, points:, :] = squared


def fold_body(first_ref, second_ref, kept_ref, sent_ref):
    for half, ref in enumerate((kept_ref, sent_ref)):
        for i in range(ref.shape[0]):
            ref[i] = first_ref[2 * i + half] + second_ref[2 * i + half]


def total_body(scale, first_ref, second_ref, gradient_ref, misfit_ref):
    points = gradient_ref.shape[1]
    total = first_ref[0] + second_ref[0]
    gradient_ref[0] = total[:points]
    misfit_ref[...] = total[points : points + 1, :1] * scale


def call(body, out_shape, operands, limit=SMALL_LIMIT, **options):
    vmem = pl.BlockSpec(memory_space=pltpu.VMEM)
    options.setdefault("in_specs", [vmem] * len(operands))
    return pl.pallas_call(
        body,
        out_shape=out_shape,
        out_specs=jax.tree.map(lambda _: vmem, out_shape),
        compiler_params=pltpu.CompilerParams(vmem_limit_bytes=limit),
        **options,
    )(*operands)


def local(model, kernel, observed, weights):
    n_sens, n_par = lax.axis_size("sens"), lax.axis_size("par")
    sensors, points, steps = kernel.shape
    vectors = n_sens * model.shape[0]
    near, far = levels(n_par, vectors)
    of_block = vectors // near
    lags = 256 // points
    rows = vectors * steps // n_par
    flops = 2 * vectors * sensors * points * steps * steps // near
    cost = pl.CostEstimate(flops=flops, bytes_accessed=2 * kernel.size, transcendentals=0)
    vmem, hbm = pl.BlockSpec(memory_space=pltpu.VMEM), pl.BlockSpec(memory_space=pltpu.HBM)

    def struct(shape, dtype):
        return jax.ShapeDtypeStruct(shape, dtype)

    n_x = max(1, n_sens.bit_length() - 1)
    part_steps = steps // n_x
    held, models, xs = model, [model], []
    for level in range(n_x):
        if level > 0:
            models[1], xs[-1] = lax.optimization_barrier((models[1], xs[-1]))
            held = call(join_body, struct((2 * held.shape[0],) + model.shape[1:], model.dtype), models)
        models = [held, swap(held, "sens", held.shape[0])]
        xs.append(
            call(
                functools.partial(turn_body, level * part_steps),
                struct((part_steps, points, sensors), kernel.dtype),
                (kernel,),
                VMEM_LIMIT,
                scratch_shapes=[
                    pltpu.VMEM((sensors * points, part_steps), jnp.float32),
                    pltpu.VMEM((part_steps * points, sensors), jnp.float32),
                ],
                cost_estimate=pl.CostEstimate(flops=0, bytes_accessed=4 * kernel.size, transcendentals=0),
            )
        )

    def forward(away):
        scratch = [
            pltpu.VMEM((vectors, points, steps), jnp.float32),
            pltpu.VMEM((of_block, lags * points, steps), jnp.float32),
            pltpu.VMEM((of_block, steps, lags * points), jnp.bfloat16),
            pltpu.VMEM((of_block * steps, sensors), jnp.float32),
        ]
        operands = [*models, *xs]
        specs = [vmem] * len(operands)
        if away == 0:
            scratch += [
                pltpu.VMEM((sensors, steps), jnp.float32),
                pltpu.VMEM((1, sensors), jnp.float32),
                pltpu.SemaphoreType.DMA((2,)),
            ]
            operands += [observed, weights[None, :]]
            specs += [hbm] * 2
            out = struct((far * rows + WEIGHT_ROWS, sensors), jnp.float32)
        else:
            out = struct((far * rows, sensors), jnp.bfloat16)
        return call(
            functools.partial(forward_body, away, near, far, lags, len(models), len(xs)),
            out,
            operands,
            VMEM_LIMIT,
            in_specs=specs,
            scratch_shapes=scratch,
            cost_estimate=cost,
        )

    terms = [swap(forward(away), "par", away) for away in range(1, near)]
    own, *sent = call(
        functools.partial(middle_body, near, far),
        [struct((rows + WEIGHT_ROWS, sensors), jnp.float32)] + [struct((rows, sensors), jnp.bfloat16)] * (far - 1),
        (forward(0), *terms),
    )
    terms = [swap(sent[b - 1], "par", b * near) for b in range(far - 1, 0, -1)]
    residual = call(residual_body, struct((rows + EXTRA_ROWS, sensors), jnp.bfloat16), (own, *terms))
    parts = [swap(residual, "par", b * near) for b in range(far - 1, 0, -1)]
    block = call(
        join_body, struct((far * (rows + EXTRA_ROWS), sensors), jnp.bfloat16), (residual, *parts[::-1])
    )
    others = [swap(block, "par", away) for away in range(1, near)]

    scratch = [
        pltpu.VMEM((of_block, lags * sensors, steps), jnp.bfloat16),
        pltpu.VMEM((of_block * steps, sensors), jnp.float32),
    ]
    left, own = call(
        functools.partial(adjoint_own_body, far, lags),
        [
            struct((steps // lags * points, lags * sensors), jnp.bfloat16),
            struct((of_block, points, steps), jnp.float32),
        ],
        (block, *xs),
        VMEM_LIMIT,
        scratch_shapes=scratch,
        cost_estimate=cost,
    )
    pair = [struct((vectors // 2, points + MISFIT_ROWS, steps), jnp.float32)] * 2
    kept, sent = call(
        functools.partial(adjoint_rest_body, far, lags),
        pair,
        (own, left, block, *others),
        VMEM_LIMIT,
        scratch_shapes=[pltpu.VMEM((vectors, points, steps), jnp.float32)] + scratch,
        cost_estimate=cost,
    )
    step = 1
    while kept.shape[0] > 1:
        pair = [struct((kept.shape[0] // 2,) + kept.shape[1:], jnp.float32)] * 2
        kept, sent = call(fold_body, pair, (kept, swap(sent, "sens", step)))
        step *= 2
    entries = vectors * sensors * n_sens * steps
    gradient, misfit = call(
        functools.partial(total_body, 0.5 / entries),
        [struct((1, points, steps), jnp.float32), struct((1, 1), jnp.float32)],
        (kept, swap(sent, "sens", step)),
    )
    return (gradient, misfit[0, 0])


def solution(mesh):
    return jax.shard_map(
        local,
        mesh=mesh,
        in_specs=(P("sens", "par", None), P("sens", "par", None), P(None, "sens", None), P("sens")),
        out_specs=(P("sens", "par", None), P()),
        check_vma=False,
    )
```

```python
import functools

import jax
import jax.numpy as jnp
from jax import lax
from jax.experimental import pallas as pl
from jax.experimental.pallas import tpu as pltpu
from jax.sharding import PartitionSpec as P

EXTRA_ROWS = 16
WEIGHT_ROWS = 8
MISFIT_ROWS = 8
VMEM_LIMIT = 24 * 1024 * 1024
SMALL_LIMIT = 4 * 1024 * 1024


def swap(value, axis, step):
    return lax.ppermute(value, axis, [(i, i ^ step) for i in range(lax.axis_size(axis))])


def levels(size, vectors):
    near = 1
    while near * near * 4 <= size and near * 2 <= vectors:
        near *= 2
    return near, size // near


def turn_body(kernel_ref, out_ref, turned_ref, *parts):
    steps, points, sensors = out_ref.shape
    count = steps // len(parts)
    for i, rows_ref in enumerate(parts):
        lags = slice(i * count, (i + 1) * count)
        rows_ref[...] = kernel_ref[:, :, lags].astype(jnp.float32).reshape(sensors * points, count)
        for p in range(points):
            plane = rows_ref[pl.ds(p, sensors, stride=points), :]
            turned_ref[pl.ds(i * count * points + p, count, stride=points), :] = plane.T
        turned = turned_ref[i * count * points : (i + 1) * count * points, :]
        out_ref[lags] = turned.reshape(count, points, sensors).astype(jnp.bfloat16)


def forward_body(away, near, far, lags, n_models, n_x, *refs):
    models, xs, refs = refs[:n_models], refs[n_models : n_models + n_x], refs[n_models + n_x :]
    part_steps, points, sensors = xs[0].shape
    steps = part_steps * n_x
    me, j = lax.axis_index("sens"), lax.axis_index("par")
    place, block = j // near, lax.rem(j, near) ^ away
    if away == 0:
        observed_ref, weights_ref, out_ref, all_ref, ut_ref, u_ref, acc_ref, seen_ref, scale_ref, sems = refs
        outs = [out_ref]
    else:
        outs, (all_ref, ut_ref, u_ref, acc_ref) = refs[:-4], refs[-4:]
    vectors, of_block = all_ref.shape[0], u_ref.shape[0]
    rows = of_block * steps // far
    if away == 0:
        first = (block * far + place) * rows
        fetch_seen = pltpu.make_async_copy(observed_ref.at[me ^ (first // steps)], seen_ref, sems.at[0])
        fetch_scale = pltpu.make_async_copy(weights_ref, scale_ref, sems.at[1])
        fetch_seen.start()
        fetch_scale.start()
    lane = lax.broadcasted_iota(jnp.int32, (points, steps), 1)
    for v in range(vectors):
        ref = models[v * n_models // vectors]
        all_ref[v] = ref[v % ref.shape[0]].astype(jnp.float32)
    for v in range(of_block):
        series = all_ref[block * of_block + v]
        for kl in range(lags):
            moved = series if kl == 0 else jnp.where(lane >= kl, pltpu.roll(series, kl, 1), 0.0)
            ut_ref[v, kl * points : (kl + 1) * points, :] = moved
        u_ref[v] = ut_ref[v].T.astype(jnp.bfloat16)
    for k0 in range(0, steps, 2 * lags):
        left = steps - k0
        x_ref, at = xs[k0 // part_steps], k0 % part_steps
        pair = [x_ref[k : k + lags].reshape(lags * points, sensors) for k in (at, at + lags)]
        some = u_ref[:, :left, :].reshape(of_block * left, lags * points)
        term = jnp.dot(some, jnp.concatenate(pair, axis=1), preferred_element_type=jnp.float32)
        for v in range(of_block):
            at, end = v * steps, (v + 1) * steps
            part = term[v * left : (v + 1) * left]
            if k0 == 0:
                acc_ref[at:end, :] = part[:, :sensors]
            else:
                acc_ref[at + k0 : end, :] += part[:, :sensors]
            acc_ref[at + k0 + lags : end, :] += part[: left - lags, sensors:]
    for b in range(far):
        there = pl.multiple_of((place ^ b) * rows, rows)
        ref, at = outs[b * len(outs) // far], b % (far // len(outs)) * rows
        ref[at : at + rows, :] = acc_ref[pl.ds(there, rows), :].astype(ref.dtype)
    if away == 0:
        fetch_seen.wait()
        fetch_scale.wait()
        ut_ref[0, :, :sensors] = seen_ref[...].T
        out_ref[:rows, :] -= ut_ref[0, pl.ds(pl.multiple_of(first % steps, rows), rows), :sensors]
        out_ref[far * rows :, :] = jnp.broadcast_to(scale_ref[...], (WEIGHT_ROWS, sensors))


def middle_body(near, start, count, own_ref, *refs):
    terms, outs = refs[: near - 1], refs[near - 1 :]
    rows = terms[0].shape[0] // count
    for i, ref in enumerate(outs):
        part = own_ref[(start + i) * rows : (start + i + 1) * rows, :]
        for term in terms:
            part += term[i * rows : (i + 1) * rows, :].astype(jnp.float32)
        ref[:rows, :] = part.astype(ref.dtype)
    if start == 0:
        outs[0][rows:, :] = own_ref[own_ref.shape[0] - WEIGHT_ROWS :, :]


def three_parts(value):
    high = value.astype(jnp.bfloat16).astype(jnp.float32)
    rest = value - high
    middle = rest.astype(jnp.bfloat16).astype(jnp.float32)
    low = rest - middle
    row = lax.broadcasted_iota(jnp.int32, (EXTRA_ROWS, value.shape[1]), 0)
    parts = jnp.where(row == 0, high, jnp.where(row == 1, middle, jnp.where(row == 2, low, 0.0)))
    return parts.astype(jnp.bfloat16)


def residual_body(own_ref, *refs):
    terms, out_ref = refs[:-1], refs[-1]
    rows, sensors = terms[0].shape
    mismatch = own_ref[:rows, :]
    for term in terms:
        mismatch += term[...].astype(jnp.float32)
    weighted = own_ref[rows : rows + 1, :] * mismatch
    out_ref[:rows, :] = weighted.astype(jnp.bfloat16)
    squared = jnp.sum(weighted * mismatch, axis=0, keepdims=True)
    out_ref[rows:, :] = three_parts(squared)


def join_body(*refs):
    parts, out_ref = refs[:-1], refs[-1]
    rows = parts[0].shape[0] - EXTRA_ROWS
    extra = 0.0
    for i, part in enumerate(parts):
        out_ref[i * rows : (i + 1) * rows, :] = part[:rows, :]
        extra += part[rows:, :].astype(jnp.float32)
    out_ref[len(parts) * rows :, :] = three_parts(jnp.sum(extra, axis=0, keepdims=True))


def adjoint_terms(groups, left_ref, r_ref, all_ref, far, lags, points):
    of_block, _, steps = r_ref.shape
    sensors = all_ref.shape[1]
    rows = of_block * steps // far
    place = lax.axis_index("par") // (lax.axis_size("par") // far)
    for b in range(far):
        there = pl.multiple_of((place ^ b) * rows, rows)
        ref, at = groups[b * len(groups) // far], b % (far // len(groups)) * rows
        all_ref[pl.ds(there, rows), :] = ref[at : at + rows, :].astype(jnp.float32)
    lane = lax.broadcasted_iota(jnp.int32, (sensors, steps), 1)
    lane_p = lax.broadcasted_iota(jnp.int32, (points, steps), 1)
    for v in range(of_block):
        series = all_ref[v * steps : (v + 1) * steps, :].T
        for d in range(lags):
            moved = series
            if d > 0:
                moved = jnp.where(lane < steps - d, pltpu.roll(series, steps - d, 1), 0.0)
            r_ref[v, d * sensors : (d + 1) * sensors, :] = moved.astype(jnp.bfloat16)
        terms = jnp.dot(left_ref[...], r_ref[v], preferred_element_type=jnp.float32)
        total = terms[:points]
        for c in range(1, steps // lags):
            moved = pltpu.roll(terms[c * points : (c + 1) * points], steps - c * lags, 1)
            total += jnp.where(lane_p < steps - c * lags, moved, 0.0)
        yield v, total


def adjoint_own_body(far, lags, n_groups, *refs):
    groups, xs, (left_ref, own_ref, r_ref, all_ref) = refs[:n_groups], refs[n_groups:-4], refs[-4:]
    part_steps, points, sensors = xs[0].shape
    for d in range(lags):
        for c in range(len(xs) * part_steps // lags):
            k = c * lags + d
            left_ref[c * points : (c + 1) * points, d * sensors : (d + 1) * sensors] = xs[k // part_steps][k % part_steps]
    for v, total in adjoint_terms(groups, left_ref, r_ref, all_ref, far, lags, points):
        own_ref[v] = total


def adjoint_rest_body(near, far, lags, n_groups, own_ref, left_ref, *refs):
    groups, outs, (slots_ref, r_ref, all_ref) = refs[: near * n_groups], refs[near * n_groups : -3], refs[-3:]
    of_block, points, steps = own_ref.shape
    lanes = outs[0].shape[1]
    block = lax.rem(lax.axis_index("par"), near)
    extra = 0.0
    for ref in groups:
        extra += ref[ref.shape[0] - EXTRA_ROWS :, :].astype(jnp.float32)
    squared = jnp.full((MISFIT_ROWS, lanes), jnp.sum(extra), jnp.float32)
    for v in range(of_block):
        slots_ref[block * of_block + v] = own_ref[v]
    for away in range(1, near):
        some = groups[away * n_groups : (away + 1) * n_groups]
        for v, total in adjoint_terms(some, left_ref, r_ref, all_ref, far, lags, points):
            slots_ref[(block ^ away) * of_block + v] = total
    for v, ref in enumerate(outs):
        for i in range(steps // lanes):
            ref[i * points : (i + 1) * points, :] = slots_ref[v, :, i * lanes : (i + 1) * lanes]
        ref[steps // lanes * points :, :] = squared


def total_body(scale, *refs):
    terms, (gradient_ref, misfit_ref) = refs[:-2], refs[-2:]
    _, points, steps = gradient_ref.shape
    lanes = terms[0].shape[1]
    total = terms[0][...]
    for term in terms[1:]:
        total += term[...]
    for i in range(steps // lanes):
        gradient_ref[0, :, i * lanes : (i + 1) * lanes] = total[i * points : (i + 1) * points]
    at = steps // lanes * points
    misfit_ref[...] = total[at : at + 1, :1] * scale


def call(body, out_shape, operands, limit=SMALL_LIMIT, **options):
    vmem = pl.BlockSpec(memory_space=pltpu.VMEM)
    options.setdefault("in_specs", [vmem] * len(operands))
    return pl.pallas_call(
        body,
        out_shape=out_shape,
        out_specs=jax.tree.map(lambda _: vmem, out_shape),
        compiler_params=pltpu.CompilerParams(vmem_limit_bytes=limit),
        **options,
    )(*operands)


def local(model, kernel, observed, weights):
    n_sens, n_par = lax.axis_size("sens"), lax.axis_size("par")
    sensors, points, steps = kernel.shape
    vectors = n_sens * model.shape[0]
    near, far = levels(n_par, vectors)
    of_block = vectors // near
    n_groups = min(2, far)
    slots = far // n_groups
    lags = 256 // points
    rows = vectors * steps // n_par
    lanes = min(128, steps)
    flops = 2 * vectors * sensors * points * steps * steps // near
    cost = pl.CostEstimate(flops=flops, bytes_accessed=2 * kernel.size, transcendentals=0)
    vmem, hbm = pl.BlockSpec(memory_space=pltpu.VMEM), pl.BlockSpec(memory_space=pltpu.HBM)

    def struct(shape, dtype):
        return jax.ShapeDtypeStruct(shape, dtype)

    models = [model] + [swap(model, "sens", step) for step in range(1, n_sens)]
    xs = [
        call(
            turn_body,
            struct((steps, points, sensors), kernel.dtype),
            (kernel,),
            VMEM_LIMIT,
            scratch_shapes=[
                pltpu.VMEM((steps * points, sensors), jnp.float32),
            ]
            + [pltpu.VMEM((sensors * points, lanes), jnp.float32)] * (steps // lanes),
            cost_estimate=pl.CostEstimate(flops=0, bytes_accessed=6 * kernel.size, transcendentals=0),
        )
    ]

    def forward(away):
        scratch = [
            pltpu.VMEM((vectors, points, steps), jnp.float32),
            pltpu.VMEM((of_block, lags * points, steps), jnp.float32),
            pltpu.VMEM((of_block, steps, lags * points), jnp.bfloat16),
            pltpu.VMEM((of_block * steps, sensors), jnp.float32),
        ]
        operands = [*models, *xs]
        specs = [vmem] * len(operands)
        if away == 0:
            scratch += [
                pltpu.VMEM((sensors, steps), jnp.float32),
                pltpu.VMEM((1, sensors), jnp.float32),
                pltpu.SemaphoreType.DMA((2,)),
            ]
            operands += [observed, weights[None, :]]
            specs += [hbm] * 2
            out = struct((far * rows + WEIGHT_ROWS, sensors), jnp.float32)
        else:
            out = [struct((slots * rows, sensors), jnp.bfloat16)] * n_groups
        return call(
            functools.partial(forward_body, away, near, far, lags, len(models), len(xs)),
            out,
            operands,
            VMEM_LIMIT,
            in_specs=specs,
            scratch_shapes=scratch,
            cost_estimate=cost,
        )

    sent = [forward(away) for away in range(1, near)]
    crossed = [[swap(some[g], "par", away) for away, some in enumerate(sent, 1)] for g in range(n_groups - 1, -1, -1)]
    sums = forward(0)
    terms = []
    for g, some in zip(range(n_groups - 1, -1, -1), crossed):
        outs = [struct((rows, sensors), jnp.bfloat16)] * slots
        if g == 0:
            outs[0] = struct((rows + WEIGHT_ROWS, sensors), jnp.float32)
        outs = call(functools.partial(middle_body, near, g * slots, slots), outs, (sums, *some))
        if g == 0:
            own, *outs = outs
        first = far - len(terms) - 1
        terms += [swap(out, "par", b * near) for b, out in zip(range(first, 0, -1), outs[::-1])]
    residual = call(residual_body, struct((rows + EXTRA_ROWS, sensors), jnp.bfloat16), (own, *terms))
    parts = [residual] + [swap(residual, "par", b * near) for b in range(1, far)]
    joined = struct((slots * rows + EXTRA_ROWS, sensors), jnp.bfloat16)
    groups = [call(join_body, joined, parts[g * slots : (g + 1) * slots]) for g in range(n_groups)]
    others = [[swap(group, "par", away) for group in groups] for away in range(1, near)]

    scratch = [
        pltpu.VMEM((of_block, lags * sensors, steps), jnp.bfloat16),
        pltpu.VMEM((of_block * steps, sensors), jnp.float32),
    ]
    left, own = call(
        functools.partial(adjoint_own_body, far, lags, n_groups),
        [
            struct((steps // lags * points, lags * sensors), jnp.bfloat16),
            struct((of_block, points, steps), jnp.float32),
        ],
        (*groups, *xs),
        VMEM_LIMIT,
        scratch_shapes=scratch,
        cost_estimate=cost,
    )
    partials = call(
        functools.partial(adjoint_rest_body, near, far, lags, n_groups),
        [struct((steps // lanes * points + MISFIT_ROWS, lanes), jnp.float32)] * vectors,
        (own, left, *groups, *[group for some in others for group in some]),
        VMEM_LIMIT,
        scratch_shapes=[pltpu.VMEM((vectors, points, steps), jnp.float32)] + scratch,
        cost_estimate=cost,
    )
    received = [swap(partials[step], "sens", step) for step in range(n_sens - 1, 0, -1)]
    entries = vectors * sensors * n_sens * steps
    gradient, misfit = call(
        functools.partial(total_body, 0.5 / entries),
        [struct((1, points, steps), jnp.float32), struct((1, 1), jnp.float32)],
        (partials[0], *received),
    )
    return (gradient, misfit[0, 0])


def solution(mesh):
    return jax.shard_map(
        local,
        mesh=mesh,
        in_specs=(P("sens", "par", None), P("sens", "par", None), P(None, "sens", None), P("sens")),
        out_specs=(P("sens", "par", None), P()),
        check_vma=False,
    )
```

```python
import functools

import jax
import jax.numpy as jnp
from jax import lax
from jax.experimental import pallas as pl
from jax.experimental.pallas import tpu as pltpu
from jax.sharding import PartitionSpec as P

EXTRA_ROWS = 16
WEIGHT_ROWS = 8
MISFIT_ROWS = 8
VMEM_LIMIT = 24 * 1024 * 1024
SMALL_LIMIT = 4 * 1024 * 1024


def swap(value, axis, step):
    return lax.ppermute(value, axis, [(i, i ^ step) for i in range(lax.axis_size(axis))])


def levels(size, vectors):
    near = 1
    while near * near * 4 <= size and near * 2 <= vectors:
        near *= 2
    return near, size // near


def turn_body(kernel_ref, out_ref, turned_ref, *parts):
    steps, points, sensors = out_ref.shape
    count = steps // len(parts)
    first = kernel_ref.shape[2] - steps
    for i, rows_ref in enumerate(parts):
        lags = slice(i * count, (i + 1) * count)
        some = kernel_ref[:, :, first + i * count : first + (i + 1) * count]
        rows_ref[...] = some.astype(jnp.float32).reshape(sensors * points, count)
        for p in range(points):
            plane = rows_ref[pl.ds(p, sensors, stride=points), :]
            turned_ref[pl.ds(i * count * points + p, count, stride=points), :] = plane.T
        turned = turned_ref[i * count * points : (i + 1) * count * points, :]
        out_ref[lags] = turned.reshape(count, points, sensors).astype(jnp.bfloat16)


def forward_body(away, near, far, lags, n_models, n_x, *refs):
    models, xs, refs = refs[:n_models], refs[n_models : n_models + n_x], refs[n_models + n_x :]
    points, sensors = xs[0].shape[1:]
    ks = [(x_ref, k) for x_ref in xs for k in range(x_ref.shape[0])]
    steps = len(ks)
    me, j = lax.axis_index("sens"), lax.axis_index("par")
    place, block = j // near, lax.rem(j, near) ^ away
    if away == 0:
        observed_ref, weights_ref, out_ref, all_ref, ut_ref, u_ref, acc_ref, seen_ref, scale_ref, sems = refs
        outs = [out_ref]
    else:
        outs, (all_ref, ut_ref, u_ref, acc_ref) = refs[:-4], refs[-4:]
    vectors, of_block = all_ref.shape[0], u_ref.shape[0]
    rows = of_block * steps // far
    if away == 0:
        first = (block * far + place) * rows
        fetch_seen = pltpu.make_async_copy(observed_ref.at[me ^ (first // steps)], seen_ref, sems.at[0])
        fetch_scale = pltpu.make_async_copy(weights_ref, scale_ref, sems.at[1])
        fetch_seen.start()
        fetch_scale.start()
    lane = lax.broadcasted_iota(jnp.int32, (points, steps), 1)
    for v in range(vectors):
        ref = models[v * n_models // vectors]
        all_ref[v] = ref[v % ref.shape[0]].astype(jnp.float32)
    for v in range(of_block):
        series = all_ref[block * of_block + v]
        for kl in range(lags):
            moved = series if kl == 0 else jnp.where(lane >= kl, pltpu.roll(series, kl, 1), 0.0)
            ut_ref[v, kl * points : (kl + 1) * points, :] = moved
        u_ref[v] = ut_ref[v].T.astype(jnp.bfloat16)
    for k0 in range(0, steps, 2 * lags):
        left = steps - k0
        x_ref, at = ks[k0]
        pair = [x_ref[k : k + lags].reshape(lags * points, sensors) for k in (at, at + lags)]
        some = u_ref[:, :left, :].reshape(of_block * left, lags * points)
        term = jnp.dot(some, jnp.concatenate(pair, axis=1), preferred_element_type=jnp.float32)
        for v in range(of_block):
            at, end = v * steps, (v + 1) * steps
            part = term[v * left : (v + 1) * left]
            if k0 == 0:
                acc_ref[at:end, :] = part[:, :sensors]
            else:
                acc_ref[at + k0 : end, :] += part[:, :sensors]
            acc_ref[at + k0 + lags : end, :] += part[: left - lags, sensors:]
    for b in range(far):
        there = pl.multiple_of((place ^ b) * rows, rows)
        ref, at = outs[b * len(outs) // far], b % (far // len(outs)) * rows
        ref[at : at + rows, :] = acc_ref[pl.ds(there, rows), :].astype(ref.dtype)
    if away == 0:
        fetch_seen.wait()
        fetch_scale.wait()
        ut_ref[0, :, :sensors] = seen_ref[...].T
        out_ref[:rows, :] -= ut_ref[0, pl.ds(pl.multiple_of(first % steps, rows), rows), :sensors]
        out_ref[far * rows :, :] = jnp.broadcast_to(scale_ref[...], (WEIGHT_ROWS, sensors))


def middle_body(near, start, count, own_ref, *refs):
    terms, outs = refs[: near - 1], refs[near - 1 :]
    rows = terms[0].shape[0] // count
    for i, ref in enumerate(outs):
        part = own_ref[(start + i) * rows : (start + i + 1) * rows, :]
        for term in terms:
            part += term[i * rows : (i + 1) * rows, :].astype(jnp.float32)
        ref[:rows, :] = part.astype(ref.dtype)
    if start == 0:
        outs[0][rows:, :] = own_ref[own_ref.shape[0] - WEIGHT_ROWS :, :]


def three_parts(value):
    high = value.astype(jnp.bfloat16).astype(jnp.float32)
    rest = value - high
    middle = rest.astype(jnp.bfloat16).astype(jnp.float32)
    low = rest - middle
    row = lax.broadcasted_iota(jnp.int32, (EXTRA_ROWS, value.shape[1]), 0)
    parts = jnp.where(row == 0, high, jnp.where(row == 1, middle, jnp.where(row == 2, low, 0.0)))
    return parts.astype(jnp.bfloat16)


def residual_body(own_ref, *refs):
    terms, out_ref = refs[:-1], refs[-1]
    rows, sensors = terms[0].shape
    mismatch = own_ref[:rows, :]
    for term in terms:
        mismatch += term[...].astype(jnp.float32)
    weighted = own_ref[rows : rows + 1, :] * mismatch
    out_ref[:rows, :] = weighted.astype(jnp.bfloat16)
    squared = jnp.sum(weighted * mismatch, axis=0, keepdims=True)
    out_ref[rows:, :] = three_parts(squared)


def join_body(*refs):
    parts, out_ref = refs[:-1], refs[-1]
    rows = parts[0].shape[0] - EXTRA_ROWS
    extra = 0.0
    for i, part in enumerate(parts):
        out_ref[i * rows : (i + 1) * rows, :] = part[:rows, :]
        extra += part[rows:, :].astype(jnp.float32)
    out_ref[len(parts) * rows :, :] = three_parts(jnp.sum(extra, axis=0, keepdims=True))


def adjoint_terms(group_ref, start, left_ref, r_ref, all_ref, slots, lags, points):
    of_group, _, steps = r_ref.shape
    sensors = all_ref.shape[1]
    rows = of_group * steps // slots
    near, _ = levels(lax.axis_size("par"), lax.axis_size("sens"))
    place = lax.axis_index("par") // near
    group = (place ^ start) // slots
    for b in range(slots):
        there = pl.multiple_of(((place ^ (start + b)) - group * slots) * rows, rows)
        all_ref[pl.ds(there, rows), :] = group_ref[b * rows : (b + 1) * rows, :].astype(jnp.float32)
    lane = lax.broadcasted_iota(jnp.int32, (sensors, steps), 1)
    lane_p = lax.broadcasted_iota(jnp.int32, (points, steps), 1)
    for v in range(of_group):
        series = all_ref[v * steps : (v + 1) * steps, :].T
        for d in range(lags):
            moved = series
            if d > 0:
                moved = jnp.where(lane < steps - d, pltpu.roll(series, steps - d, 1), 0.0)
            r_ref[v, d * sensors : (d + 1) * sensors, :] = moved.astype(jnp.bfloat16)
        terms = jnp.dot(left_ref[...], r_ref[v], preferred_element_type=jnp.float32)
        total = terms[:points]
        for c in range(1, steps // lags):
            moved = pltpu.roll(terms[c * points : (c + 1) * points], steps - c * lags, 1)
            total += jnp.where(lane_p < steps - c * lags, moved, 0.0)
        yield group * of_group + v, total


def left_body(lags, *refs):
    xs, left_ref = refs[:-1], refs[-1]
    points, sensors = xs[0].shape[1:]
    ks = [(x_ref, k) for x_ref in xs for k in range(x_ref.shape[0])]
    for k, (x_ref, at) in enumerate(ks):
        c, d = divmod(k, lags)
        left_ref[c * points : (c + 1) * points, d * sensors : (d + 1) * sensors] = x_ref[at]


def adjoint_piece_body(start, slots, lags, group_ref, left_ref, out_ref, r_ref, all_ref):
    points = out_ref.shape[1]
    for v, (_, total) in enumerate(adjoint_terms(group_ref, start, left_ref, r_ref, all_ref, slots, lags, points)):
        out_ref[v] = total


def adjoint_last_body(near, slots, lags, n_groups, *refs):
    done, refs = refs[: near * n_groups - 1], refs[near * n_groups - 1 :]
    left_ref, groups, refs = refs[0], refs[1 : 1 + near * n_groups], refs[1 + near * n_groups :]
    outs, (slots_ref, r_ref, all_ref) = refs[:-3], refs[-3:]
    of_group, points, steps = done[0].shape
    of_block, lanes = of_group * n_groups, outs[0].shape[1]
    j = lax.axis_index("par")
    place, block = j // near, lax.rem(j, near)
    extra = 0.0
    for ref in groups:
        extra += ref[ref.shape[0] - EXTRA_ROWS :, :].astype(jnp.float32)
    squared = jnp.full((MISFIT_ROWS, lanes), jnp.sum(extra), jnp.float32)
    for i, ref in enumerate(done):
        away, group = i // n_groups, (place ^ (i % n_groups * slots)) // slots
        for v in range(of_group):
            slots_ref[(block ^ away) * of_block + group * of_group + v] = ref[v]
    start = (n_groups - 1) * slots
    for v, total in adjoint_terms(groups[-1], start, left_ref, r_ref, all_ref, slots, lags, points):
        slots_ref[(block ^ (near - 1)) * of_block + v] = total
    for v, ref in enumerate(outs):
        for i in range(steps // lanes):
            ref[i * points : (i + 1) * points, :] = slots_ref[v, :, i * lanes : (i + 1) * lanes]
        ref[steps // lanes * points :, :] = squared


def total_body(scale, *refs):
    terms, (gradient_ref, misfit_ref) = refs[:-2], refs[-2:]
    _, points, steps = gradient_ref.shape
    lanes = terms[0].shape[1]
    total = terms[0][...]
    for term in terms[1:]:
        total += term[...]
    for i in range(steps // lanes):
        gradient_ref[0, :, i * lanes : (i + 1) * lanes] = total[i * points : (i + 1) * points]
    at = steps // lanes * points
    misfit_ref[...] = total[at : at + 1, :1] * scale


def call(body, out_shape, operands, limit=SMALL_LIMIT, **options):
    vmem = pl.BlockSpec(memory_space=pltpu.VMEM)
    options.setdefault("in_specs", [vmem] * len(operands))
    return pl.pallas_call(
        body,
        out_shape=out_shape,
        out_specs=jax.tree.map(lambda _: vmem, out_shape),
        compiler_params=pltpu.CompilerParams(vmem_limit_bytes=limit),
        **options,
    )(*operands)


def local(model, kernel, observed, weights):
    n_sens, n_par = lax.axis_size("sens"), lax.axis_size("par")
    sensors, points, steps = kernel.shape
    vectors = n_sens * model.shape[0]
    near, far = levels(n_par, vectors)
    of_block = vectors // near
    n_groups = 2 if of_block % 2 == 0 and far % 2 == 0 else 1
    slots = far // n_groups
    lags = 256 // points
    rows = vectors * steps // n_par
    lanes = min(128, steps)
    flops = 2 * vectors * sensors * points * steps * steps // near
    cost = pl.CostEstimate(flops=flops, bytes_accessed=2 * kernel.size, transcendentals=0)
    piece_cost = pl.CostEstimate(flops=flops // n_groups, bytes_accessed=2 * kernel.size, transcendentals=0)
    vmem, hbm = pl.BlockSpec(memory_space=pltpu.VMEM), pl.BlockSpec(memory_space=pltpu.HBM)

    def struct(shape, dtype):
        return jax.ShapeDtypeStruct(shape, dtype)

    models = [model] + [swap(model, "sens", step) for step in range(1, n_sens)]
    half = steps - steps // lanes // 2 * lanes
    xs = [
        call(
            turn_body,
            struct((count, points, sensors), kernel.dtype),
            (some,),
            VMEM_LIMIT,
            scratch_shapes=[pltpu.VMEM((count * points, sensors), jnp.float32)]
            + [pltpu.VMEM((sensors * points, lanes), jnp.float32)] * (count // lanes),
            cost_estimate=pl.CostEstimate(flops=0, bytes_accessed=3 * kernel.size, transcendentals=0),
        )
        for count, some in ((half, kernel[:, :, :half]), (steps - half, kernel))
        if count > 0
    ]

    def forward(away):
        scratch = [
            pltpu.VMEM((vectors, points, steps), jnp.float32),
            pltpu.VMEM((of_block, lags * points, steps), jnp.float32),
            pltpu.VMEM((of_block, steps, lags * points), jnp.bfloat16),
            pltpu.VMEM((of_block * steps, sensors), jnp.float32),
        ]
        operands = [*models, *xs]
        specs = [vmem] * len(operands)
        if away == 0:
            scratch += [
                pltpu.VMEM((sensors, steps), jnp.float32),
                pltpu.VMEM((1, sensors), jnp.float32),
                pltpu.SemaphoreType.DMA((2,)),
            ]
            operands += [observed, weights[None, :]]
            specs += [hbm] * 2
            out = struct((far * rows + WEIGHT_ROWS, sensors), jnp.float32)
        else:
            out = [struct((slots * rows, sensors), jnp.bfloat16)] * n_groups
        return call(
            functools.partial(forward_body, away, near, far, lags, len(models), len(xs)),
            out,
            operands,
            VMEM_LIMIT,
            in_specs=specs,
            scratch_shapes=scratch,
            cost_estimate=cost,
        )

    sent = [forward(away) for away in range(1, near)]
    crossed = [[swap(some[g], "par", away) for away, some in enumerate(sent, 1)] for g in range(n_groups - 1, -1, -1)]
    sums = forward(0)
    terms = []
    for g, some in zip(range(n_groups - 1, -1, -1), crossed):
        outs = [struct((rows, sensors), jnp.bfloat16)] * slots
        if g == 0:
            outs[0] = struct((rows + WEIGHT_ROWS, sensors), jnp.float32)
        outs = call(functools.partial(middle_body, near, g * slots, slots), outs, (sums, *some))
        if g == 0:
            own, *outs = outs
        first = far - len(terms) - 1
        terms += [swap(out, "par", b * near) for b, out in zip(range(first, 0, -1), outs[::-1])]
    residual = call(residual_body, struct((rows + EXTRA_ROWS, sensors), jnp.bfloat16), (own, *terms))
    parts = [residual] + [swap(residual, "par", b * near) for b in range(1, far)]
    joined = struct((slots * rows + EXTRA_ROWS, sensors), jnp.bfloat16)
    groups = [call(join_body, joined, parts[g * slots : (g + 1) * slots]) for g in range(n_groups)]
    others = [[swap(group, "par", away) for group in groups] for away in range(1, near)]

    of_group = of_block // n_groups
    scratch = [
        pltpu.VMEM((of_group, lags * sensors, steps), jnp.bfloat16),
        pltpu.VMEM((of_group * steps, sensors), jnp.float32),
    ]
    left = call(
        functools.partial(left_body, lags),
        struct((steps // lags * points, lags * sensors), jnp.bfloat16),
        xs,
        VMEM_LIMIT,
        cost_estimate=pl.CostEstimate(flops=0, bytes_accessed=kernel.size, transcendentals=0),
    )
    every = groups + [group for some in others for group in some]
    done = [
        call(
            functools.partial(adjoint_piece_body, i % n_groups * slots, slots, lags),
            struct((of_group, points, steps), jnp.float32),
            (group, left),
            VMEM_LIMIT,
            scratch_shapes=scratch,
            cost_estimate=piece_cost,
        )
        for i, group in enumerate(every[:-1])
    ]
    partials = call(
        functools.partial(adjoint_last_body, near, slots, lags, n_groups),
        [struct((steps // lanes * points + MISFIT_ROWS, lanes), jnp.float32)] * vectors,
        (*done, left, *every),
        VMEM_LIMIT,
        scratch_shapes=[pltpu.VMEM((vectors, points, steps), jnp.float32)] + scratch,
        cost_estimate=piece_cost,
    )
    received = [swap(partials[step], "sens", step) for step in range(n_sens - 1, 0, -1)]
    entries = vectors * sensors * n_sens * steps
    gradient, misfit = call(
        functools.partial(total_body, 0.5 / entries),
        [struct((1, points, steps), jnp.float32), struct((1, 1), jnp.float32)],
        (partials[0], *received),
    )
    return (gradient, misfit[0, 0])


def solution(mesh):
    return jax.shard_map(
        local,
        mesh=mesh,
        in_specs=(P("sens", "par", None), P("sens", "par", None), P(None, "sens", None), P("sens")),
        out_specs=(P("sens", "par", None), P()),
        check_vma=False,
    )
```

```python
import functools

import jax
import jax.numpy as jnp
from jax import lax
from jax.experimental import pallas as pl
from jax.experimental.pallas import tpu as pltpu
from jax.sharding import PartitionSpec as P

EXTRA_ROWS = 16
WEIGHT_ROWS = 8
MISFIT_ROWS = 8
VMEM_LIMIT = 24 * 1024 * 1024
SMALL_LIMIT = 4 * 1024 * 1024


def swap(value, axis, step):
    return lax.ppermute(value, axis, [(i, i ^ step) for i in range(lax.axis_size(axis))])


def levels(size, vectors):
    near = 1
    while near * near * 4 <= size and near * 2 <= vectors:
        near *= 2
    return near, size // near


def turn_body(kernel_ref, out_ref, turned_ref, *parts):
    steps, points, sensors = out_ref.shape
    count = steps // len(parts)
    first = kernel_ref.shape[2] - steps
    for i, rows_ref in enumerate(parts):
        lags = slice(i * count, (i + 1) * count)
        some = kernel_ref[:, :, first + i * count : first + (i + 1) * count]
        rows_ref[...] = some.astype(jnp.float32).reshape(sensors * points, count)
        for p in range(points):
            plane = rows_ref[pl.ds(p, sensors, stride=points), :]
            turned_ref[pl.ds(i * count * points + p, count, stride=points), :] = plane.T
        turned = turned_ref[i * count * points : (i + 1) * count * points, :]
        out_ref[lags] = turned.reshape(count, points, sensors).astype(jnp.bfloat16)


def forward_body(away, start, slots, near, lags, n_models, n_x, *refs):
    models, xs, refs = refs[:n_models], refs[n_models : n_models + n_x], refs[n_models + n_x :]
    points, sensors = xs[0].shape[1:]
    ks = [(x_ref, k) for x_ref in xs for k in range(x_ref.shape[0])]
    steps = len(ks)
    me, j = lax.axis_index("sens"), lax.axis_index("par")
    place, block = j // near, lax.rem(j, near) ^ away
    if away == 0:
        observed_ref, weights_ref, out_ref, all_ref, ut_ref, u_ref, acc_ref, seen_ref, scale_ref, sems = refs
    else:
        out_ref, all_ref, ut_ref, u_ref, acc_ref = refs
    vectors, of_group = all_ref.shape[0], u_ref.shape[0]
    rows = of_group * steps // slots
    group = (place ^ start) // slots
    if away == 0:
        first = (block * slots + place) * rows
        fetch_seen = pltpu.make_async_copy(observed_ref.at[me ^ (first // steps)], seen_ref, sems.at[0])
        fetch_scale = pltpu.make_async_copy(weights_ref, scale_ref, sems.at[1])
        fetch_seen.start()
        fetch_scale.start()
    lane = lax.broadcasted_iota(jnp.int32, (points, steps), 1)
    for v in range(vectors):
        ref = models[v * n_models // vectors]
        all_ref[v] = ref[v % ref.shape[0]].astype(jnp.float32)
    for v in range(of_group):
        series = all_ref[block * (vectors // near) + group * of_group + v]
        for kl in range(lags):
            moved = series if kl == 0 else jnp.where(lane >= kl, pltpu.roll(series, kl, 1), 0.0)
            ut_ref[v, kl * points : (kl + 1) * points, :] = moved
        u_ref[v] = ut_ref[v].T.astype(jnp.bfloat16)
    for k0 in range(0, steps, 2 * lags):
        left = steps - k0
        x_ref, at = ks[k0]
        pair = [x_ref[k : k + lags].reshape(lags * points, sensors) for k in (at, at + lags)]
        some = u_ref[:, :left, :].reshape(of_group * left, lags * points)
        term = jnp.dot(some, jnp.concatenate(pair, axis=1), preferred_element_type=jnp.float32)
        for v in range(of_group):
            at, end = v * steps, (v + 1) * steps
            part = term[v * left : (v + 1) * left]
            if k0 == 0:
                acc_ref[at:end, :] = part[:, :sensors]
            else:
                acc_ref[at + k0 : end, :] += part[:, :sensors]
            acc_ref[at + k0 + lags : end, :] += part[: left - lags, sensors:]
    for b in range(slots):
        there = pl.multiple_of(((place ^ (start + b)) - group * slots) * rows, rows)
        out_ref[b * rows : (b + 1) * rows, :] = acc_ref[pl.ds(there, rows), :].astype(out_ref.dtype)
    if away == 0:
        fetch_seen.wait()
        fetch_scale.wait()
        ut_ref[0, :, :sensors] = seen_ref[...].T
        out_ref[:rows, :] -= ut_ref[0, pl.ds(pl.multiple_of(first % steps, rows), rows), :sensors]
        out_ref[slots * rows :, :] = jnp.broadcast_to(scale_ref[...], (WEIGHT_ROWS, sensors))


def middle_body(near, start, count, own_ref, *refs):
    terms, outs = refs[: near - 1], refs[near - 1 :]
    rows = terms[0].shape[0] // count
    for i, ref in enumerate(outs):
        part = own_ref[(start + i) * rows : (start + i + 1) * rows, :]
        for term in terms:
            part += term[i * rows : (i + 1) * rows, :].astype(jnp.float32)
        ref[:rows, :] = part.astype(ref.dtype)
    if start == 0:
        outs[0][rows:, :] = own_ref[own_ref.shape[0] - WEIGHT_ROWS :, :]


def three_parts(value):
    high = value.astype(jnp.bfloat16).astype(jnp.float32)
    rest = value - high
    middle = rest.astype(jnp.bfloat16).astype(jnp.float32)
    low = rest - middle
    row = lax.broadcasted_iota(jnp.int32, (EXTRA_ROWS, value.shape[1]), 0)
    parts = jnp.where(row == 0, high, jnp.where(row == 1, middle, jnp.where(row == 2, low, 0.0)))
    return parts.astype(jnp.bfloat16)


def residual_body(own_ref, *refs):
    terms, out_ref = refs[:-1], refs[-1]
    rows, sensors = terms[0].shape
    mismatch = own_ref[:rows, :]
    for term in terms:
        mismatch += term[...].astype(jnp.float32)
    weighted = own_ref[rows : rows + 1, :] * mismatch
    out_ref[:rows, :] = weighted.astype(jnp.bfloat16)
    squared = jnp.sum(weighted * mismatch, axis=0, keepdims=True)
    out_ref[rows:, :] = three_parts(squared)


def join_body(*refs):
    parts, out_ref = refs[:-1], refs[-1]
    rows = parts[0].shape[0] - EXTRA_ROWS
    extra = 0.0
    for i, part in enumerate(parts):
        out_ref[i * rows : (i + 1) * rows, :] = part[:rows, :]
        extra += part[rows:, :].astype(jnp.float32)
    out_ref[len(parts) * rows :, :] = three_parts(jnp.sum(extra, axis=0, keepdims=True))


def adjoint_terms(group_ref, start, left_ref, r_ref, all_ref, slots, lags, points):
    of_group, _, steps = r_ref.shape
    sensors = all_ref.shape[1]
    rows = of_group * steps // slots
    near, _ = levels(lax.axis_size("par"), lax.axis_size("sens"))
    place = lax.axis_index("par") // near
    group = (place ^ start) // slots
    for b in range(slots):
        there = pl.multiple_of(((place ^ (start + b)) - group * slots) * rows, rows)
        all_ref[pl.ds(there, rows), :] = group_ref[b * rows : (b + 1) * rows, :].astype(jnp.float32)
    lane = lax.broadcasted_iota(jnp.int32, (sensors, steps), 1)
    lane_p = lax.broadcasted_iota(jnp.int32, (points, steps), 1)
    for v in range(of_group):
        series = all_ref[v * steps : (v + 1) * steps, :].T
        for d in range(lags):
            moved = series
            if d > 0:
                moved = jnp.where(lane < steps - d, pltpu.roll(series, steps - d, 1), 0.0)
            r_ref[v, d * sensors : (d + 1) * sensors, :] = moved.astype(jnp.bfloat16)
        terms = jnp.dot(left_ref[...], r_ref[v], preferred_element_type=jnp.float32)
        total = terms[:points]
        for c in range(1, steps // lags):
            moved = pltpu.roll(terms[c * points : (c + 1) * points], steps - c * lags, 1)
            total += jnp.where(lane_p < steps - c * lags, moved, 0.0)
        yield group * of_group + v, total


def left_body(lags, *refs):
    xs, left_ref = refs[:-1], refs[-1]
    points, sensors = xs[0].shape[1:]
    ks = [(x_ref, k) for x_ref in xs for k in range(x_ref.shape[0])]
    for k, (x_ref, at) in enumerate(ks):
        c, d = divmod(k, lags)
        left_ref[c * points : (c + 1) * points, d * sensors : (d + 1) * sensors] = x_ref[at]


def adjoint_piece_body(start, slots, lags, group_ref, left_ref, out_ref, r_ref, all_ref):
    points = out_ref.shape[1]
    for v, (_, total) in enumerate(adjoint_terms(group_ref, start, left_ref, r_ref, all_ref, slots, lags, points)):
        out_ref[v] = total


def adjoint_last_body(near, slots, lags, n_groups, *refs):
    done, refs = refs[: near * n_groups - 1], refs[near * n_groups - 1 :]
    left_ref, groups, refs = refs[0], refs[1 : 1 + near * n_groups], refs[1 + near * n_groups :]
    outs, (slots_ref, r_ref, all_ref) = refs[:-3], refs[-3:]
    of_group, points, steps = done[0].shape
    of_block, lanes = of_group * n_groups, outs[0].shape[1]
    j = lax.axis_index("par")
    place, block = j // near, lax.rem(j, near)
    extra = 0.0
    for ref in groups:
        extra += ref[ref.shape[0] - EXTRA_ROWS :, :].astype(jnp.float32)
    squared = jnp.full((MISFIT_ROWS, lanes), jnp.sum(extra), jnp.float32)
    for i, ref in enumerate(done):
        away, group = i // n_groups, (place ^ (i % n_groups * slots)) // slots
        for v in range(of_group):
            slots_ref[(block ^ away) * of_block + group * of_group + v] = ref[v]
    start = (n_groups - 1) * slots
    for v, total in adjoint_terms(groups[-1], start, left_ref, r_ref, all_ref, slots, lags, points):
        slots_ref[(block ^ (near - 1)) * of_block + v] = total
    for v, ref in enumerate(outs):
        for i in range(steps // lanes):
            ref[i * points : (i + 1) * points, :] = slots_ref[v, :, i * lanes : (i + 1) * lanes]
        ref[steps // lanes * points :, :] = squared


def total_body(scale, *refs):
    terms, (gradient_ref, misfit_ref) = refs[:-2], refs[-2:]
    _, points, steps = gradient_ref.shape
    lanes = terms[0].shape[1]
    total = terms[0][...]
    for term in terms[1:]:
        total += term[...]
    for i in range(steps // lanes):
        gradient_ref[0, :, i * lanes : (i + 1) * lanes] = total[i * points : (i + 1) * points]
    at = steps // lanes * points
    misfit_ref[...] = total[at : at + 1, :1] * scale


def call(body, out_shape, operands, limit=SMALL_LIMIT, **options):
    vmem = pl.BlockSpec(memory_space=pltpu.VMEM)
    options.setdefault("in_specs", [vmem] * len(operands))
    return pl.pallas_call(
        body,
        out_shape=out_shape,
        out_specs=jax.tree.map(lambda _: vmem, out_shape),
        compiler_params=pltpu.CompilerParams(vmem_limit_bytes=limit),
        **options,
    )(*operands)


def local(model, kernel, observed, weights):
    n_sens, n_par = lax.axis_size("sens"), lax.axis_size("par")
    sensors, points, steps = kernel.shape
    vectors = n_sens * model.shape[0]
    near, far = levels(n_par, vectors)
    of_block = vectors // near
    n_groups = 2 if of_block % 2 == 0 and far % 2 == 0 else 1
    slots = far // n_groups
    lags = 256 // points
    rows = vectors * steps // n_par
    lanes = min(128, steps)
    flops = 2 * vectors * sensors * points * steps * steps // near
    cost = pl.CostEstimate(flops=flops, bytes_accessed=2 * kernel.size, transcendentals=0)
    piece_cost = pl.CostEstimate(flops=flops // n_groups, bytes_accessed=2 * kernel.size, transcendentals=0)
    vmem, hbm = pl.BlockSpec(memory_space=pltpu.VMEM), pl.BlockSpec(memory_space=pltpu.HBM)

    def struct(shape, dtype):
        return jax.ShapeDtypeStruct(shape, dtype)

    models = [model] + [swap(model, "sens", step) for step in range(1, n_sens)]
    half = steps - steps // lanes // 2 * lanes
    xs = [jnp.transpose(kernel[:, :, :half], (2, 1, 0))]
    if half < steps:
        xs.append(
            call(
                turn_body,
                struct((steps - half, points, sensors), kernel.dtype),
                (kernel,),
                VMEM_LIMIT,
                scratch_shapes=[pltpu.VMEM(((steps - half) * points, sensors), jnp.float32)]
                + [pltpu.VMEM((sensors * points, lanes), jnp.float32)] * ((steps - half) // lanes),
                cost_estimate=pl.CostEstimate(flops=0, bytes_accessed=3 * kernel.size, transcendentals=0),
            )
        )

    def forward(away, start, count):
        of_part = of_block * count // far
        scratch = [
            pltpu.VMEM((vectors, points, steps), jnp.float32),
            pltpu.VMEM((of_part, lags * points, steps), jnp.float32),
            pltpu.VMEM((of_part, steps, lags * points), jnp.bfloat16),
            pltpu.VMEM((of_part * steps, sensors), jnp.float32),
        ]
        operands = [*models, *xs]
        specs = [vmem] * len(operands)
        if away == 0:
            scratch += [
                pltpu.VMEM((sensors, steps), jnp.float32),
                pltpu.VMEM((1, sensors), jnp.float32),
                pltpu.SemaphoreType.DMA((2,)),
            ]
            operands += [observed, weights[None, :]]
            specs += [hbm] * 2
            out = struct((count * rows + WEIGHT_ROWS, sensors), jnp.float32)
        else:
            out = struct((count * rows, sensors), jnp.bfloat16)
        return call(
            functools.partial(forward_body, away, start, count, near, lags, len(models), len(xs)),
            out,
            operands,
            VMEM_LIMIT,
            in_specs=specs,
            scratch_shapes=scratch,
            cost_estimate=cost if away == 0 else piece_cost,
        )

    crossed = [
        [swap(forward(away, g * slots, slots), "par", away) for away in range(1, near)]
        for g in range(n_groups - 1, -1, -1)
    ]
    sums = forward(0, 0, far)
    terms = []
    for g, some in zip(range(n_groups - 1, -1, -1), crossed):
        outs = [struct((rows, sensors), jnp.bfloat16)] * slots
        if g == 0:
            outs[0] = struct((rows + WEIGHT_ROWS, sensors), jnp.float32)
        outs = call(functools.partial(middle_body, near, g * slots, slots), outs, (sums, *some))
        if g == 0:
            own, *outs = outs
        first = far - len(terms) - 1
        terms += [swap(out, "par", b * near) for b, out in zip(range(first, 0, -1), outs[::-1])]
    residual = call(residual_body, struct((rows + EXTRA_ROWS, sensors), jnp.bfloat16), (own, *terms))
    parts = [residual] + [swap(residual, "par", b * near) for b in range(1, far)]
    joined = struct((slots * rows + EXTRA_ROWS, sensors), jnp.bfloat16)
    groups = [call(join_body, joined, parts[g * slots : (g + 1) * slots]) for g in range(n_groups)]
    others = [[swap(group, "par", away) for group in groups] for away in range(1, near)]

    of_group = of_block // n_groups
    scratch = [
        pltpu.VMEM((of_group, lags * sensors, steps), jnp.bfloat16),
        pltpu.VMEM((of_group * steps, sensors), jnp.float32),
    ]
    left = call(
        functools.partial(left_body, lags),
        struct((steps // lags * points, lags * sensors), jnp.bfloat16),
        xs,
        VMEM_LIMIT,
        cost_estimate=pl.CostEstimate(flops=0, bytes_accessed=kernel.size, transcendentals=0),
    )
    every = groups + [group for some in others for group in some]
    done = [
        call(
            functools.partial(adjoint_piece_body, i % n_groups * slots, slots, lags),
            struct((of_group, points, steps), jnp.float32),
            (group, left),
            VMEM_LIMIT,
            scratch_shapes=scratch,
            cost_estimate=piece_cost,
        )
        for i, group in enumerate(every[:-1])
    ]
    partials = call(
        functools.partial(adjoint_last_body, near, slots, lags, n_groups),
        [struct((steps // lanes * points + MISFIT_ROWS, lanes), jnp.float32)] * vectors,
        (*done, left, *every),
        VMEM_LIMIT,
        scratch_shapes=[pltpu.VMEM((vectors, points, steps), jnp.float32)] + scratch,
        cost_estimate=piece_cost,
    )
    received = [swap(partials[step], "sens", step) for step in range(n_sens - 1, 0, -1)]
    entries = vectors * sensors * n_sens * steps
    gradient, misfit = call(
        functools.partial(total_body, 0.5 / entries),
        [struct((1, points, steps), jnp.float32), struct((1, 1), jnp.float32)],
        (partials[0], *received),
    )
    return (gradient, misfit[0, 0])


def solution(mesh):
    return jax.shard_map(
        local,
        mesh=mesh,
        in_specs=(P("sens", "par", None), P("sens", "par", None), P(None, "sens", None), P("sens")),
        out_specs=(P("sens", "par", None), P()),
        check_vma=False,
    )
```

```python
import functools

import jax
import jax.numpy as jnp
from jax import lax
from jax.experimental import pallas as pl
from jax.experimental.pallas import tpu as pltpu
from jax.sharding import PartitionSpec as P

EXTRA_ROWS = 16
WEIGHT_ROWS = 8
MISFIT_ROWS = 8
VMEM_LIMIT = 24 * 1024 * 1024
SMALL_LIMIT = 4 * 1024 * 1024


def swap(value, axis, step):
    return lax.ppermute(value, axis, [(i, i ^ step) for i in range(lax.axis_size(axis))])


def levels(size, vectors):
    near = 1
    while near * near * 4 <= size and near * 2 <= vectors:
        near *= 2
    return near, size // near


def turn_body(kernel_ref, out_ref, turned_ref, *parts):
    steps, points, sensors = out_ref.shape
    count = steps // len(parts)
    first = kernel_ref.shape[2] - steps
    for i, rows_ref in enumerate(parts):
        lags = slice(i * count, (i + 1) * count)
        some = kernel_ref[:, :, first + i * count : first + (i + 1) * count]
        rows_ref[...] = some.astype(jnp.float32).reshape(sensors * points, count)
        for p in range(points):
            plane = rows_ref[pl.ds(p, sensors, stride=points), :]
            turned_ref[pl.ds(i * count * points + p, count, stride=points), :] = plane.T
        turned = turned_ref[i * count * points : (i + 1) * count * points, :]
        out_ref[lags] = turned.reshape(count, points, sensors).astype(jnp.bfloat16)


def forward_body(away, start, slots, near, lags, n_models, n_x, *refs):
    models, xs, refs = refs[:n_models], refs[n_models : n_models + n_x], refs[n_models + n_x :]
    points, sensors = xs[0].shape[1:]
    ks = [(x_ref, k) for x_ref in xs for k in range(x_ref.shape[0])]
    steps = len(ks)
    me, j = lax.axis_index("sens"), lax.axis_index("par")
    place, block = j // near, lax.rem(j, near) ^ away
    if away == 0:
        observed_ref, weights_ref, out_ref, all_ref, ut_ref, u_ref, acc_ref, seen_ref, scale_ref, sems = refs
    else:
        out_ref, all_ref, ut_ref, u_ref, acc_ref = refs
    vectors, of_group = all_ref.shape[0], u_ref.shape[0]
    rows = of_group * steps // slots
    group = (place ^ start) // slots
    if away == 0:
        first = (block * slots + place) * rows
        fetch_seen = pltpu.make_async_copy(observed_ref.at[me ^ (first // steps)], seen_ref, sems.at[0])
        fetch_scale = pltpu.make_async_copy(weights_ref, scale_ref, sems.at[1])
        fetch_seen.start()
        fetch_scale.start()
    lane = lax.broadcasted_iota(jnp.int32, (points, steps), 1)
    for v in range(vectors):
        ref = models[v * n_models // vectors]
        all_ref[v] = ref[v % ref.shape[0]].astype(jnp.float32)
    for v in range(of_group):
        series = all_ref[block * (vectors // near) + group * of_group + v]
        for kl in range(lags):
            moved = series if kl == 0 else jnp.where(lane >= kl, pltpu.roll(series, kl, 1), 0.0)
            ut_ref[v, kl * points : (kl + 1) * points, :] = moved
        u_ref[v] = ut_ref[v].T.astype(jnp.bfloat16)
    for k0 in range(0, steps, 2 * lags):
        left = steps - k0
        x_ref, at = ks[k0]
        pair = [x_ref[k : k + lags].reshape(lags * points, sensors) for k in (at, at + lags)]
        some = u_ref[:, :left, :].reshape(of_group * left, lags * points)
        term = jnp.dot(some, jnp.concatenate(pair, axis=1), preferred_element_type=jnp.float32)
        for v in range(of_group):
            at, end = v * steps, (v + 1) * steps
            part = term[v * left : (v + 1) * left]
            if k0 == 0:
                acc_ref[at:end, :] = part[:, :sensors]
            else:
                acc_ref[at + k0 : end, :] += part[:, :sensors]
            acc_ref[at + k0 + lags : end, :] += part[: left - lags, sensors:]
    for b in range(slots):
        there = pl.multiple_of(((place ^ (start + b)) - group * slots) * rows, rows)
        out_ref[b * rows : (b + 1) * rows, :] = acc_ref[pl.ds(there, rows), :].astype(out_ref.dtype)
    if away == 0:
        fetch_seen.wait()
        fetch_scale.wait()
        ut_ref[0, :, :sensors] = seen_ref[...].T
        out_ref[:rows, :] -= ut_ref[0, pl.ds(pl.multiple_of(first % steps, rows), rows), :sensors]
        out_ref[slots * rows :, :] = jnp.broadcast_to(scale_ref[...], (WEIGHT_ROWS, sensors))


def middle_body(near, start, count, own_ref, *refs):
    terms, outs = refs[: near - 1], refs[near - 1 :]
    rows = terms[0].shape[0] // count
    for i, ref in enumerate(outs):
        part = own_ref[(start + i) * rows : (start + i + 1) * rows, :]
        for term in terms:
            part += term[i * rows : (i + 1) * rows, :].astype(jnp.float32)
        ref[:rows, :] = part.astype(ref.dtype)
    if start == 0:
        outs[0][rows:, :] = own_ref[own_ref.shape[0] - WEIGHT_ROWS :, :]


def three_parts(value):
    high = value.astype(jnp.bfloat16).astype(jnp.float32)
    rest = value - high
    middle = rest.astype(jnp.bfloat16).astype(jnp.float32)
    low = rest - middle
    row = lax.broadcasted_iota(jnp.int32, (EXTRA_ROWS, value.shape[1]), 0)
    parts = jnp.where(row == 0, high, jnp.where(row == 1, middle, jnp.where(row == 2, low, 0.0)))
    return parts.astype(jnp.bfloat16)


def residual_body(own_ref, *refs):
    terms, out_ref = refs[:-1], refs[-1]
    rows, sensors = terms[0].shape
    mismatch = own_ref[:rows, :]
    for term in terms:
        mismatch += term[...].astype(jnp.float32)
    weighted = own_ref[rows : rows + 1, :] * mismatch
    out_ref[:rows, :] = weighted.astype(jnp.bfloat16)
    squared = jnp.sum(weighted * mismatch, axis=0, keepdims=True)
    out_ref[rows:, :] = three_parts(squared)


def join_body(*refs):
    parts, out_ref = refs[:-1], refs[-1]
    rows = parts[0].shape[0] - EXTRA_ROWS
    extra = 0.0
    for i, part in enumerate(parts):
        out_ref[i * rows : (i + 1) * rows, :] = part[:rows, :]
        extra += part[rows:, :].astype(jnp.float32)
    out_ref[len(parts) * rows :, :] = three_parts(jnp.sum(extra, axis=0, keepdims=True))


def adjoint_terms(group, start, left_ref, r_ref, all_ref, slots, lags, points):
    of_group, _, steps = r_ref.shape
    sensors = all_ref.shape[1]
    rows = of_group * steps // slots
    near, _ = levels(lax.axis_size("par"), lax.axis_size("sens"))
    place = lax.axis_index("par") // near
    index = (place ^ start) // slots
    per = slots // len(group)
    for b in range(slots):
        there = pl.multiple_of(((place ^ (start + b)) - index * slots) * rows, rows)
        at = b % per * rows
        all_ref[pl.ds(there, rows), :] = group[b // per][at : at + rows, :].astype(jnp.float32)
    lane = lax.broadcasted_iota(jnp.int32, (sensors, steps), 1)
    lane_p = lax.broadcasted_iota(jnp.int32, (points, steps), 1)
    for v in range(of_group):
        series = all_ref[v * steps : (v + 1) * steps, :].T
        for d in range(lags):
            moved = series
            if d > 0:
                moved = jnp.where(lane < steps - d, pltpu.roll(series, steps - d, 1), 0.0)
            r_ref[v, d * sensors : (d + 1) * sensors, :] = moved.astype(jnp.bfloat16)
        terms = jnp.dot(left_ref[...], r_ref[v], preferred_element_type=jnp.float32)
        total = terms[:points]
        for c in range(1, steps // lags):
            moved = pltpu.roll(terms[c * points : (c + 1) * points], steps - c * lags, 1)
            total += jnp.where(lane_p < steps - c * lags, moved, 0.0)
        yield index * of_group + v, total


def left_body(lags, *refs):
    xs, left_ref = refs[:-1], refs[-1]
    points, sensors = xs[0].shape[1:]
    ks = [(x_ref, k) for x_ref in xs for k in range(x_ref.shape[0])]
    for k, (x_ref, at) in enumerate(ks):
        c, d = divmod(k, lags)
        left_ref[c * points : (c + 1) * points, d * sensors : (d + 1) * sensors] = x_ref[at]


def adjoint_piece_body(start, slots, lags, *refs):
    group, (left_ref, out_ref, r_ref, all_ref) = refs[:-4], refs[-4:]
    points = out_ref.shape[1]
    for v, (_, total) in enumerate(adjoint_terms(group, start, left_ref, r_ref, all_ref, slots, lags, points)):
        out_ref[v] = total


def adjoint_last_body(near, slots, lags, n_groups, n_last, *refs):
    done, refs = refs[: near * n_groups - 1], refs[near * n_groups - 1 :]
    slots_ref, r_ref, all_ref = refs[-3:]
    vectors = slots_ref.shape[0]
    left_ref, groups, outs = refs[0], refs[1 : -3 - vectors], refs[-3 - vectors : -3]
    of_group, points, steps = done[0].shape
    of_block, lanes = of_group * n_groups, outs[0].shape[1]
    j = lax.axis_index("par")
    place, block = j // near, lax.rem(j, near)
    extra = 0.0
    for ref in groups:
        extra += ref[ref.shape[0] - EXTRA_ROWS :, :].astype(jnp.float32)
    squared = jnp.full((MISFIT_ROWS, lanes), jnp.sum(extra), jnp.float32)
    for i, ref in enumerate(done):
        away, group = i // n_groups, (place ^ (i % n_groups * slots)) // slots
        for v in range(of_group):
            slots_ref[(block ^ away) * of_block + group * of_group + v] = ref[v]
    start = (n_groups - 1) * slots
    for v, total in adjoint_terms(groups[-n_last:], start, left_ref, r_ref, all_ref, slots, lags, points):
        slots_ref[(block ^ (near - 1)) * of_block + v] = total
    for v, ref in enumerate(outs):
        for i in range(steps // lanes):
            ref[i * points : (i + 1) * points, :] = slots_ref[v, :, i * lanes : (i + 1) * lanes]
        ref[steps // lanes * points :, :] = squared


def total_body(scale, *refs):
    terms, (gradient_ref, misfit_ref) = refs[:-2], refs[-2:]
    _, points, steps = gradient_ref.shape
    lanes = terms[0].shape[1]
    total = terms[0][...]
    for term in terms[1:]:
        total += term[...]
    for i in range(steps // lanes):
        gradient_ref[0, :, i * lanes : (i + 1) * lanes] = total[i * points : (i + 1) * points]
    at = steps // lanes * points
    misfit_ref[...] = total[at : at + 1, :1] * scale


def call(body, out_shape, operands, limit=SMALL_LIMIT, **options):
    vmem = pl.BlockSpec(memory_space=pltpu.VMEM)
    options.setdefault("in_specs", [vmem] * len(operands))
    return pl.pallas_call(
        body,
        out_shape=out_shape,
        out_specs=jax.tree.map(lambda _: vmem, out_shape),
        compiler_params=pltpu.CompilerParams(vmem_limit_bytes=limit),
        **options,
    )(*operands)


def local(model, kernel, observed, weights):
    n_sens, n_par = lax.axis_size("sens"), lax.axis_size("par")
    sensors, points, steps = kernel.shape
    vectors = n_sens * model.shape[0]
    near, far = levels(n_par, vectors)
    of_block = vectors // near
    n_groups = 2 if of_block % 2 == 0 and far % 2 == 0 else 1
    slots = far // n_groups
    lags = 256 // points
    rows = vectors * steps // n_par
    lanes = min(128, steps)
    flops = 2 * vectors * sensors * points * steps * steps // near
    cost = pl.CostEstimate(flops=flops, bytes_accessed=2 * kernel.size, transcendentals=0)
    piece_cost = pl.CostEstimate(flops=flops // n_groups, bytes_accessed=2 * kernel.size, transcendentals=0)
    vmem, hbm = pl.BlockSpec(memory_space=pltpu.VMEM), pl.BlockSpec(memory_space=pltpu.HBM)

    def struct(shape, dtype):
        return jax.ShapeDtypeStruct(shape, dtype)

    models = [model] + [swap(model, "sens", step) for step in range(1, n_sens)]
    half = steps - steps // lanes // 2 * lanes
    xs = [jnp.transpose(kernel[:, :, :half], (2, 1, 0))]
    if half < steps:
        xs.append(
            call(
                turn_body,
                struct((steps - half, points, sensors), kernel.dtype),
                (kernel,),
                VMEM_LIMIT,
                scratch_shapes=[pltpu.VMEM(((steps - half) * points, sensors), jnp.float32)]
                + [pltpu.VMEM((sensors * points, lanes), jnp.float32)] * ((steps - half) // lanes),
                cost_estimate=pl.CostEstimate(flops=0, bytes_accessed=3 * kernel.size, transcendentals=0),
            )
        )

    def forward(away, start, count):
        of_part = of_block * count // far
        scratch = [
            pltpu.VMEM((vectors, points, steps), jnp.float32),
            pltpu.VMEM((of_part, lags * points, steps), jnp.float32),
            pltpu.VMEM((of_part, steps, lags * points), jnp.bfloat16),
            pltpu.VMEM((of_part * steps, sensors), jnp.float32),
        ]
        operands = [*models, *xs]
        specs = [vmem] * len(operands)
        if away == 0:
            scratch += [
                pltpu.VMEM((sensors, steps), jnp.float32),
                pltpu.VMEM((1, sensors), jnp.float32),
                pltpu.SemaphoreType.DMA((2,)),
            ]
            operands += [observed, weights[None, :]]
            specs += [hbm] * 2
            out = struct((count * rows + WEIGHT_ROWS, sensors), jnp.float32)
        else:
            out = struct((count * rows, sensors), jnp.bfloat16)
        return call(
            functools.partial(forward_body, away, start, count, near, lags, len(models), len(xs)),
            out,
            operands,
            VMEM_LIMIT,
            in_specs=specs,
            scratch_shapes=scratch,
            cost_estimate=cost if away == 0 else piece_cost,
        )

    crossed = [
        [swap(forward(away, g * slots, slots), "par", away) for away in range(1, near)]
        for g in range(n_groups - 1, -1, -1)
    ]
    sums = forward(0, 0, far)
    terms = []
    for g, some in zip(range(n_groups - 1, -1, -1), crossed):
        outs = [struct((rows, sensors), jnp.bfloat16)] * slots
        if g == 0:
            outs[0] = struct((rows + WEIGHT_ROWS, sensors), jnp.float32)
        outs = call(functools.partial(middle_body, near, g * slots, slots), outs, (sums, *some))
        if g == 0:
            own, *outs = outs
        first = far - len(terms) - 1
        terms += [swap(out, "par", b * near) for b, out in zip(range(first, 0, -1), outs[::-1])]
    residual = call(residual_body, struct((rows + EXTRA_ROWS, sensors), jnp.bfloat16), (own, *terms))
    parts = [residual] + [swap(residual, "par", b * near) for b in range(1, far)]
    n_last = 2 if slots % 2 == 0 else 1
    starts = [*range(0, far - slots, slots), *range(far - slots, far, slots // n_last), far]
    pieces = []
    for start, end in zip(starts, starts[1:]):
        joined = struct(((end - start) * rows + EXTRA_ROWS, sensors), jnp.bfloat16)
        pieces.append(parts[start] if end - start == 1 else call(join_body, joined, parts[start:end]))
    groups = [[piece] for piece in pieces[:-n_last]] + [pieces[-n_last:]]
    others = [[[swap(piece, "par", away) for piece in group] for group in groups] for away in range(1, near)]

    of_group = of_block // n_groups
    scratch = [
        pltpu.VMEM((of_group, lags * sensors, steps), jnp.bfloat16),
        pltpu.VMEM((of_group * steps, sensors), jnp.float32),
    ]
    left = call(
        functools.partial(left_body, lags),
        struct((steps // lags * points, lags * sensors), jnp.bfloat16),
        xs,
        VMEM_LIMIT,
        cost_estimate=pl.CostEstimate(flops=0, bytes_accessed=kernel.size, transcendentals=0),
    )
    every = groups + [group for some in others for group in some]
    done = [
        call(
            functools.partial(adjoint_piece_body, i % n_groups * slots, slots, lags),
            struct((of_group, points, steps), jnp.float32),
            (*group, left),
            VMEM_LIMIT,
            scratch_shapes=scratch,
            cost_estimate=piece_cost,
        )
        for i, group in enumerate(every[:-1])
    ]
    partials = call(
        functools.partial(adjoint_last_body, near, slots, lags, n_groups, n_last),
        [struct((steps // lanes * points + MISFIT_ROWS, lanes), jnp.float32)] * vectors,
        (*done, left, *[piece for group in every for piece in group]),
        VMEM_LIMIT,
        scratch_shapes=[pltpu.VMEM((vectors, points, steps), jnp.float32)] + scratch,
        cost_estimate=piece_cost,
    )
    received = [swap(partials[step], "sens", step) for step in range(n_sens - 1, 0, -1)]
    entries = vectors * sensors * n_sens * steps
    gradient, misfit = call(
        functools.partial(total_body, 0.5 / entries),
        [struct((1, points, steps), jnp.float32), struct((1, 1), jnp.float32)],
        (partials[0], *received),
    )
    return (gradient, misfit[0, 0])


def solution(mesh):
    return jax.shard_map(
        local,
        mesh=mesh,
        in_specs=(P("sens", "par", None), P("sens", "par", None), P(None, "sens", None), P("sens")),
        out_specs=(P("sens", "par", None), P()),
        check_vma=False,
    )
```

```python
import functools

import jax
import jax.numpy as jnp
from jax import lax
from jax.experimental import pallas as pl
from jax.experimental.pallas import tpu as pltpu
from jax.sharding import PartitionSpec as P

EXTRA_ROWS = 16
WEIGHT_ROWS = 8
MISFIT_ROWS = 8
VMEM_LIMIT = 24 * 1024 * 1024
SMALL_LIMIT = 4 * 1024 * 1024


def swap(value, axis, step):
    return lax.ppermute(value, axis, [(i, i ^ step) for i in range(lax.axis_size(axis))])


def levels(size, vectors):
    near = 1
    while near * near * 4 <= size and near * 2 <= vectors:
        near *= 2
    return near, size // near


def turn_body(kernel_ref, out_ref, turned_ref, *parts):
    steps, points, sensors = out_ref.shape
    count = steps // len(parts)
    first = kernel_ref.shape[2] - steps
    for i, rows_ref in enumerate(parts):
        lags = slice(i * count, (i + 1) * count)
        some = kernel_ref[:, :, first + i * count : first + (i + 1) * count]
        rows_ref[...] = some.astype(jnp.float32).reshape(sensors * points, count)
        for p in range(points):
            plane = rows_ref[pl.ds(p, sensors, stride=points), :]
            turned_ref[pl.ds(i * count * points + p, count, stride=points), :] = plane.T
        turned = turned_ref[i * count * points : (i + 1) * count * points, :]
        out_ref[lags] = turned.reshape(count, points, sensors).astype(jnp.bfloat16)


def forward_body(away, start, slots, near, lags, n_models, n_x, *refs):
    models, xs, refs = refs[:n_models], refs[n_models : n_models + n_x], refs[n_models + n_x :]
    points, sensors = xs[0].shape[1:]
    ks = [(x_ref, k) for x_ref in xs for k in range(x_ref.shape[0])]
    steps = len(ks)
    me, j = lax.axis_index("sens"), lax.axis_index("par")
    place, block = j // near, lax.rem(j, near) ^ away
    if away == 0:
        observed_ref, weights_ref, out_ref, all_ref, ut_ref, u_ref, acc_ref, seen_ref, scale_ref, sems = refs
    else:
        out_ref, all_ref, ut_ref, u_ref, acc_ref = refs
    vectors, of_group = all_ref.shape[0], u_ref.shape[0]
    rows = of_group * steps // slots
    group = (place ^ start) // slots
    if away == 0:
        first = (block * slots + place) * rows
        fetch_seen = pltpu.make_async_copy(observed_ref.at[me ^ (first // steps)], seen_ref, sems.at[0])
        fetch_scale = pltpu.make_async_copy(weights_ref, scale_ref, sems.at[1])
        fetch_seen.start()
        fetch_scale.start()
    lane = lax.broadcasted_iota(jnp.int32, (points, steps), 1)
    for v in range(vectors):
        ref = models[v * n_models // vectors]
        all_ref[v] = ref[v % ref.shape[0]].astype(jnp.float32)
    for v in range(of_group):
        series = all_ref[block * (vectors // near) + group * of_group + v]
        for kl in range(lags):
            moved = series if kl == 0 else jnp.where(lane >= kl, pltpu.roll(series, kl, 1), 0.0)
            ut_ref[v, kl * points : (kl + 1) * points, :] = moved
        u_ref[v] = ut_ref[v].T.astype(jnp.bfloat16)
    for k0 in range(0, steps, 2 * lags):
        left = steps - k0
        x_ref, at = ks[k0]
        pair = [x_ref[k : k + lags].reshape(lags * points, sensors) for k in (at, at + lags)]
        some = u_ref[:, :left, :].reshape(of_group * left, lags * points)
        term = jnp.dot(some, jnp.concatenate(pair, axis=1), preferred_element_type=jnp.float32)
        for v in range(of_group):
            at, end = v * steps, (v + 1) * steps
            part = term[v * left : (v + 1) * left]
            if k0 == 0:
                acc_ref[at:end, :] = part[:, :sensors]
            else:
                acc_ref[at + k0 : end, :] += part[:, :sensors]
            acc_ref[at + k0 + lags : end, :] += part[: left - lags, sensors:]
    for b in range(slots):
        there = pl.multiple_of(((place ^ (start + b)) - group * slots) * rows, rows)
        out_ref[b * rows : (b + 1) * rows, :] = acc_ref[pl.ds(there, rows), :].astype(out_ref.dtype)
    if away == 0:
        fetch_seen.wait()
        fetch_scale.wait()
        ut_ref[0, :, :sensors] = seen_ref[...].T
        out_ref[:rows, :] -= ut_ref[0, pl.ds(pl.multiple_of(first % steps, rows), rows), :sensors]
        out_ref[slots * rows :, :] = jnp.broadcast_to(scale_ref[...], (WEIGHT_ROWS, sensors))


def middle_body(near, start, count, own_ref, *refs):
    terms, outs = refs[: near - 1], refs[near - 1 :]
    rows = terms[0].shape[0] // count
    for i, ref in enumerate(outs):
        part = own_ref[(start + i) * rows : (start + i + 1) * rows, :]
        for term in terms:
            part += term[i * rows : (i + 1) * rows, :].astype(jnp.float32)
        ref[:rows, :] = part.astype(ref.dtype)
    if start == 0:
        outs[0][rows:, :] = own_ref[own_ref.shape[0] - WEIGHT_ROWS :, :]


def three_parts(value):
    high = value.astype(jnp.bfloat16).astype(jnp.float32)
    rest = value - high
    middle = rest.astype(jnp.bfloat16).astype(jnp.float32)
    low = rest - middle
    row = lax.broadcasted_iota(jnp.int32, (EXTRA_ROWS, value.shape[1]), 0)
    parts = jnp.where(row == 0, high, jnp.where(row == 1, middle, jnp.where(row == 2, low, 0.0)))
    return parts.astype(jnp.bfloat16)


def residual_body(own_ref, *refs):
    terms, out_ref = refs[:-1], refs[-1]
    rows, sensors = terms[0].shape
    mismatch = own_ref[:rows, :]
    for term in terms:
        mismatch += term[...].astype(jnp.float32)
    weighted = own_ref[rows : rows + 1, :] * mismatch
    out_ref[:rows, :] = weighted.astype(jnp.bfloat16)
    squared = jnp.sum(weighted * mismatch, axis=0, keepdims=True)
    out_ref[rows:, :] = three_parts(squared)


def join_body(*refs):
    parts, out_ref = refs[:-1], refs[-1]
    rows = parts[0].shape[0] - EXTRA_ROWS
    extra = 0.0
    for i, part in enumerate(parts):
        out_ref[i * rows : (i + 1) * rows, :] = part[:rows, :]
        extra += part[rows:, :].astype(jnp.float32)
    out_ref[len(parts) * rows :, :] = three_parts(jnp.sum(extra, axis=0, keepdims=True))


def adjoint_terms(group, start, left_ref, r_ref, all_ref, slots, lags, points):
    of_group, _, steps = r_ref.shape
    sensors = all_ref.shape[1]
    rows = of_group * steps // slots
    near, _ = levels(lax.axis_size("par"), lax.axis_size("sens"))
    place = lax.axis_index("par") // near
    index = (place ^ start) // slots
    per = slots // len(group)
    for b in range(slots):
        there = pl.multiple_of(((place ^ (start + b)) - index * slots) * rows, rows)
        at = b % per * rows
        all_ref[pl.ds(there, rows), :] = group[b // per][at : at + rows, :].astype(jnp.float32)
    lane = lax.broadcasted_iota(jnp.int32, (sensors, steps), 1)
    lane_p = lax.broadcasted_iota(jnp.int32, (points, steps), 1)
    for v in range(of_group):
        series = all_ref[v * steps : (v + 1) * steps, :].T
        for d in range(lags):
            moved = series
            if d > 0:
                moved = jnp.where(lane < steps - d, pltpu.roll(series, steps - d, 1), 0.0)
            r_ref[v, d * sensors : (d + 1) * sensors, :] = moved.astype(jnp.bfloat16)
        terms = jnp.dot(left_ref[...], r_ref[v], preferred_element_type=jnp.float32)
        total = terms[:points]
        for c in range(1, steps // lags):
            moved = pltpu.roll(terms[c * points : (c + 1) * points], steps - c * lags, 1)
            total += jnp.where(lane_p < steps - c * lags, moved, 0.0)
        yield index * of_group + v, total


def left_body(lags, *refs):
    xs, left_ref = refs[:-1], refs[-1]
    points, sensors = xs[0].shape[1:]
    ks = [(x_ref, k) for x_ref in xs for k in range(x_ref.shape[0])]
    for k, (x_ref, at) in enumerate(ks):
        c, d = divmod(k, lags)
        left_ref[c * points : (c + 1) * points, d * sensors : (d + 1) * sensors] = x_ref[at]


def adjoint_piece_body(start, slots, lags, *refs):
    group, (left_ref, out_ref, r_ref, all_ref) = refs[:-4], refs[-4:]
    points = out_ref.shape[1]
    for v, (_, total) in enumerate(adjoint_terms(group, start, left_ref, r_ref, all_ref, slots, lags, points)):
        out_ref[v] = total


def adjoint_last_body(near, slots, lags, n_groups, n_last, *refs):
    done, refs = refs[: near * n_groups - 1], refs[near * n_groups - 1 :]
    slots_ref, r_ref, all_ref = refs[-3:]
    vectors = slots_ref.shape[0]
    left_ref, groups, outs = refs[0], refs[1 : -3 - vectors], refs[-3 - vectors : -3]
    of_group, points, steps = done[0].shape
    of_block, lanes = of_group * n_groups, outs[0].shape[1]
    j = lax.axis_index("par")
    place, block = j // near, lax.rem(j, near)
    extra = 0.0
    for ref in groups:
        extra += ref[ref.shape[0] - EXTRA_ROWS :, :].astype(jnp.float32)
    squared = jnp.full((MISFIT_ROWS, lanes), jnp.sum(extra), jnp.float32)
    for i, ref in enumerate(done):
        away, group = i // n_groups, (place ^ (i % n_groups * slots)) // slots
        for v in range(of_group):
            slots_ref[(block ^ away) * of_block + group * of_group + v] = ref[v]
    start = (n_groups - 1) * slots
    for v, total in adjoint_terms(groups[-n_last:], start, left_ref, r_ref, all_ref, slots, lags, points):
        slots_ref[(block ^ (near - 1)) * of_block + v] = total
    for v, ref in enumerate(outs):
        for i in range(steps // lanes):
            ref[i * points : (i + 1) * points, :] = slots_ref[v, :, i * lanes : (i + 1) * lanes]
        ref[steps // lanes * points :, :] = squared


def total_body(scale, *refs):
    terms, (gradient_ref, misfit_ref) = refs[:-2], refs[-2:]
    _, points, steps = gradient_ref.shape
    lanes = terms[0].shape[1]
    total = terms[0][...]
    for term in terms[1:]:
        total += term[...]
    for i in range(steps // lanes):
        gradient_ref[0, :, i * lanes : (i + 1) * lanes] = total[i * points : (i + 1) * points]
    at = steps // lanes * points
    misfit_ref[...] = total[at : at + 1, :1] * scale


def call(body, out_shape, operands, limit=SMALL_LIMIT, **options):
    vmem = pl.BlockSpec(memory_space=pltpu.VMEM)
    options.setdefault("in_specs", [vmem] * len(operands))
    return pl.pallas_call(
        body,
        out_shape=out_shape,
        out_specs=jax.tree.map(lambda _: vmem, out_shape),
        compiler_params=pltpu.CompilerParams(vmem_limit_bytes=limit),
        **options,
    )(*operands)


def local(model, kernel, observed, weights):
    n_sens, n_par = lax.axis_size("sens"), lax.axis_size("par")
    sensors, points, steps = kernel.shape
    vectors = n_sens * model.shape[0]
    near, far = levels(n_par, vectors)
    of_block = vectors // near
    n_groups = 2 if of_block % 2 == 0 and far % 2 == 0 else 1
    slots = far // n_groups
    lags = 256 // points
    rows = vectors * steps // n_par
    lanes = min(128, steps)
    flops = 2 * vectors * sensors * points * steps * steps // near
    cost = pl.CostEstimate(flops=flops, bytes_accessed=2 * kernel.size, transcendentals=0)
    piece_cost = pl.CostEstimate(flops=flops // n_groups, bytes_accessed=2 * kernel.size, transcendentals=0)
    vmem, hbm = pl.BlockSpec(memory_space=pltpu.VMEM), pl.BlockSpec(memory_space=pltpu.HBM)

    def struct(shape, dtype):
        return jax.ShapeDtypeStruct(shape, dtype)

    models = [model] + [swap(model, "sens", step) for step in range(1, n_sens)]
    half = steps - steps // lanes // 2 * lanes
    xs = [jnp.transpose(kernel[:, :, :half], (2, 1, 0))]
    if half < steps:
        xs.append(
            call(
                turn_body,
                struct((steps - half, points, sensors), kernel.dtype),
                (kernel,),
                VMEM_LIMIT,
                scratch_shapes=[pltpu.VMEM(((steps - half) * points, sensors), jnp.float32)]
                + [pltpu.VMEM((sensors * points, lanes), jnp.float32)] * ((steps - half) // lanes),
                cost_estimate=pl.CostEstimate(flops=0, bytes_accessed=3 * kernel.size, transcendentals=0),
            )
        )

    def forward(away, start, count):
        of_part = of_block * count // far
        scratch = [
            pltpu.VMEM((vectors, points, steps), jnp.float32),
            pltpu.VMEM((of_part, lags * points, steps), jnp.float32),
            pltpu.VMEM((of_part, steps, lags * points), jnp.bfloat16),
            pltpu.VMEM((of_part * steps, sensors), jnp.float32),
        ]
        operands = [*models, *xs]
        specs = [vmem] * len(operands)
        if away == 0:
            scratch += [
                pltpu.VMEM((sensors, steps), jnp.float32),
                pltpu.VMEM((1, sensors), jnp.float32),
                pltpu.SemaphoreType.DMA((2,)),
            ]
            operands += [observed, weights[None, :]]
            specs += [hbm] * 2
            out = struct((count * rows + WEIGHT_ROWS, sensors), jnp.float32)
        else:
            out = struct((count * rows, sensors), jnp.bfloat16)
        return call(
            functools.partial(forward_body, away, start, count, near, lags, len(models), len(xs)),
            out,
            operands,
            VMEM_LIMIT,
            in_specs=specs,
            scratch_shapes=scratch,
            cost_estimate=cost if away == 0 else piece_cost,
        )

    crossed = [
        [swap(forward(away, g * slots, slots), "par", away) for away in range(1, near)]
        for g in range(n_groups - 1, -1, -1)
    ]
    sums = forward(0, 0, far)
    terms = []
    for g, some in zip(range(n_groups - 1, -1, -1), crossed):
        outs = [struct((rows, sensors), jnp.bfloat16)] * slots
        if g == 0:
            outs[0] = struct((rows + WEIGHT_ROWS, sensors), jnp.float32)
        outs = call(functools.partial(middle_body, near, g * slots, slots), outs, (sums, *some))
        if g == 0:
            own, *outs = outs
        first = far - len(terms) - 1
        terms += [swap(out, "par", b * near) for b, out in zip(range(first, 0, -1), outs[::-1])]
    residual = call(residual_body, struct((rows + EXTRA_ROWS, sensors), jnp.bfloat16), (own, *terms))
    parts = [residual] + [swap(residual, "par", b * near) for b in range(1, far)]
    n_last = 2 if slots % 2 == 0 else 1
    starts = [*range(0, far - slots, slots), *range(far - slots, far, slots // n_last), far]
    pieces = []
    for start, end in zip(starts, starts[1:]):
        joined = struct(((end - start) * rows + EXTRA_ROWS, sensors), jnp.bfloat16)
        pieces.append(parts[start] if end - start == 1 else call(join_body, joined, parts[start:end]))
    groups = [[piece] for piece in pieces[:-n_last]] + [pieces[-n_last:]]

    of_group = of_block // n_groups
    scratch = [
        pltpu.VMEM((of_group, lags * sensors, steps), jnp.bfloat16),
        pltpu.VMEM((of_group * steps, sensors), jnp.float32),
    ]
    least_cost = pl.CostEstimate(flops=0, bytes_accessed=0, transcendentals=0)
    left = call(
        functools.partial(left_body, lags),
        struct((steps // lags * points, lags * sensors), jnp.bfloat16),
        xs,
        VMEM_LIMIT,
        cost_estimate=least_cost,
    )

    def adjoint_piece(i, group):
        return call(
            functools.partial(adjoint_piece_body, i % n_groups * slots, slots, lags),
            struct((of_group, points, steps), jnp.float32),
            (*group, left),
            VMEM_LIMIT,
            scratch_shapes=scratch,
            cost_estimate=least_cost if i < n_groups - 1 else cost,
        )

    done = [adjoint_piece(g, groups[g]) for g in range(n_groups - 1)]
    others = [[[swap(piece, "par", away) for piece in group] for group in groups] for away in range(1, near)]
    every = groups + [group for some in others for group in some]
    done += [adjoint_piece(i, every[i]) for i in range(len(done), len(every) - 1)]
    partials = call(
        functools.partial(adjoint_last_body, near, slots, lags, n_groups, n_last),
        [struct((steps // lanes * points + MISFIT_ROWS, lanes), jnp.float32)] * vectors,
        (*done, left, *[piece for group in every for piece in group]),
        VMEM_LIMIT,
        scratch_shapes=[pltpu.VMEM((vectors, points, steps), jnp.float32)] + scratch,
        cost_estimate=piece_cost,
    )
    received = [swap(partials[step], "sens", step) for step in range(n_sens - 1, 0, -1)]
    entries = vectors * sensors * n_sens * steps
    gradient, misfit = call(
        functools.partial(total_body, 0.5 / entries),
        [struct((1, points, steps), jnp.float32), struct((1, 1), jnp.float32)],
        (partials[0], *received),
    )
    return (gradient, misfit[0, 0])


def solution(mesh):
    return jax.shard_map(
        local,
        mesh=mesh,
        in_specs=(P("sens", "par", None), P("sens", "par", None), P(None, "sens", None), P("sens")),
        out_specs=(P("sens", "par", None), P()),
        check_vma=False,
    )
```

```python
import functools

import jax
import jax.numpy as jnp
from jax import lax
from jax.experimental import pallas as pl
from jax.experimental.pallas import tpu as pltpu
from jax.sharding import PartitionSpec as P

EXTRA_ROWS = 16
WEIGHT_ROWS = 8
VMEM_LIMIT = 24 * 1024 * 1024
SMALL_LIMIT = 4 * 1024 * 1024


def swap(value, axis, step):
    return lax.ppermute(value, axis, [(i, i ^ step) for i in range(lax.axis_size(axis))])


def levels(size, vectors):
    near = 1
    while near * near * 4 <= size and near * 2 <= vectors:
        near *= 2
    return near, size // near


def turn_body(kernel_ref, out_ref, turned_ref, *parts):
    steps, points, sensors = out_ref.shape
    count = steps // len(parts)
    first = kernel_ref.shape[2] - steps
    for i, rows_ref in enumerate(parts):
        lags = slice(i * count, (i + 1) * count)
        some = kernel_ref[:, :, first + i * count : first + (i + 1) * count]
        rows_ref[...] = some.astype(jnp.float32).reshape(sensors * points, count)
        for p in range(points):
            plane = rows_ref[pl.ds(p, sensors, stride=points), :]
            turned_ref[pl.ds(i * count * points + p, count, stride=points), :] = plane.T
        turned = turned_ref[i * count * points : (i + 1) * count * points, :]
        out_ref[lags] = turned.reshape(count, points, sensors).astype(jnp.bfloat16)


def forward_body(away, start, slots, near, lags, n_models, n_x, *refs):
    models, xs, refs = refs[:n_models], refs[n_models : n_models + n_x], refs[n_models + n_x :]
    points, sensors = xs[0].shape[1:]
    ks = [(x_ref, k) for x_ref in xs for k in range(x_ref.shape[0])]
    steps = len(ks)
    me, j = lax.axis_index("sens"), lax.axis_index("par")
    place, block = j // near, lax.rem(j, near) ^ away
    if away == 0:
        observed_ref, weights_ref, out_ref, all_ref, ut_ref, u_ref, acc_ref, seen_ref, scale_ref, sems = refs
    else:
        out_ref, all_ref, ut_ref, u_ref, acc_ref = refs
    vectors, of_group = all_ref.shape[0], u_ref.shape[0]
    rows = of_group * steps // slots
    group = (place ^ start) // slots
    if away == 0:
        first = (block * slots + place) * rows
        fetch_seen = pltpu.make_async_copy(observed_ref.at[me ^ (first // steps)], seen_ref, sems.at[0])
        fetch_scale = pltpu.make_async_copy(weights_ref, scale_ref, sems.at[1])
        fetch_seen.start()
        fetch_scale.start()
    lane = lax.broadcasted_iota(jnp.int32, (points, steps), 1)
    for v in range(vectors):
        ref = models[v * n_models // vectors]
        all_ref[v] = ref[v % ref.shape[0]].astype(jnp.float32)
    for v in range(of_group):
        series = all_ref[block * (vectors // near) + group * of_group + v]
        for kl in range(lags):
            moved = series if kl == 0 else jnp.where(lane >= kl, pltpu.roll(series, kl, 1), 0.0)
            ut_ref[v, kl * points : (kl + 1) * points, :] = moved
        u_ref[v] = ut_ref[v].T.astype(jnp.bfloat16)
    for k0 in range(0, steps, 2 * lags):
        left = steps - k0
        x_ref, at = ks[k0]
        pair = [x_ref[k : k + lags].reshape(lags * points, sensors) for k in (at, at + lags)]
        some = u_ref[:, :left, :].reshape(of_group * left, lags * points)
        term = jnp.dot(some, jnp.concatenate(pair, axis=1), preferred_element_type=jnp.float32)
        for v in range(of_group):
            at, end = v * steps, (v + 1) * steps
            part = term[v * left : (v + 1) * left]
            if k0 == 0:
                acc_ref[at:end, :] = part[:, :sensors]
            else:
                acc_ref[at + k0 : end, :] += part[:, :sensors]
            acc_ref[at + k0 + lags : end, :] += part[: left - lags, sensors:]
    for b in range(slots):
        there = pl.multiple_of(((place ^ (start + b)) - group * slots) * rows, rows)
        out_ref[b * rows : (b + 1) * rows, :] = acc_ref[pl.ds(there, rows), :].astype(out_ref.dtype)
    if away == 0:
        fetch_seen.wait()
        fetch_scale.wait()
        ut_ref[0, :, :sensors] = seen_ref[...].T
        out_ref[:rows, :] -= ut_ref[0, pl.ds(pl.multiple_of(first % steps, rows), rows), :sensors]
        out_ref[slots * rows :, :] = jnp.broadcast_to(scale_ref[...], (WEIGHT_ROWS, sensors))


def middle_body(near, start, count, own_ref, *refs):
    terms, outs = refs[: near - 1], refs[near - 1 :]
    rows = terms[0].shape[0] // count
    for i, ref in enumerate(outs):
        part = own_ref[(start + i) * rows : (start + i + 1) * rows, :]
        for term in terms:
            part += term[i * rows : (i + 1) * rows, :].astype(jnp.float32)
        ref[:rows, :] = part.astype(ref.dtype)
    if start == 0:
        outs[0][rows:, :] = own_ref[own_ref.shape[0] - WEIGHT_ROWS :, :]


def three_parts(value):
    high = value.astype(jnp.bfloat16).astype(jnp.float32)
    rest = value - high
    middle = rest.astype(jnp.bfloat16).astype(jnp.float32)
    low = rest - middle
    row = lax.broadcasted_iota(jnp.int32, (EXTRA_ROWS, value.shape[1]), 0)
    parts = jnp.where(row == 0, high, jnp.where(row == 1, middle, jnp.where(row == 2, low, 0.0)))
    return parts.astype(jnp.bfloat16)


def residual_body(own_ref, *refs):
    terms, out_ref = refs[:-1], refs[-1]
    rows, sensors = terms[0].shape
    mismatch = own_ref[:rows, :]
    for term in terms:
        mismatch += term[...].astype(jnp.float32)
    weighted = own_ref[rows : rows + 1, :] * mismatch
    out_ref[:rows, :] = weighted.astype(jnp.bfloat16)
    squared = jnp.sum(weighted * mismatch, axis=0, keepdims=True)
    out_ref[rows:, :] = three_parts(squared)


def join_body(*refs):
    parts, out_ref = refs[:-1], refs[-1]
    rows = parts[0].shape[0] - EXTRA_ROWS
    extra = 0.0
    for i, part in enumerate(parts):
        out_ref[i * rows : (i + 1) * rows, :] = part[:rows, :]
        extra += part[rows:, :].astype(jnp.float32)
    out_ref[len(parts) * rows :, :] = three_parts(jnp.sum(extra, axis=0, keepdims=True))


def adjoint_terms(group, start, left_ref, r_ref, all_ref, slots, lags, points):
    of_group, _, steps = r_ref.shape
    sensors = all_ref.shape[1]
    rows = of_group * steps // slots
    near, _ = levels(lax.axis_size("par"), lax.axis_size("sens"))
    place = lax.axis_index("par") // near
    index = (place ^ start) // slots
    per = slots // len(group)
    for b in range(slots):
        there = pl.multiple_of(((place ^ (start + b)) - index * slots) * rows, rows)
        at = b % per * rows
        all_ref[pl.ds(there, rows), :] = group[b // per][at : at + rows, :].astype(jnp.float32)
    lane = lax.broadcasted_iota(jnp.int32, (sensors, steps), 1)
    lane_p = lax.broadcasted_iota(jnp.int32, (points, steps), 1)
    for v in range(of_group):
        series = all_ref[v * steps : (v + 1) * steps, :].T
        for d in range(lags):
            moved = series
            if d > 0:
                moved = jnp.where(lane < steps - d, pltpu.roll(series, steps - d, 1), 0.0)
            r_ref[v, d * sensors : (d + 1) * sensors, :] = moved.astype(jnp.bfloat16)
        terms = jnp.dot(left_ref[...], r_ref[v], preferred_element_type=jnp.float32)
        total = terms[:points]
        for c in range(1, steps // lags):
            moved = pltpu.roll(terms[c * points : (c + 1) * points], steps - c * lags, 1)
            total += jnp.where(lane_p < steps - c * lags, moved, 0.0)
        yield index * of_group + v, total


def left_body(lags, *refs):
    xs, left_ref = refs[:-1], refs[-1]
    points, sensors = xs[0].shape[1:]
    ks = [(x_ref, k) for x_ref in xs for k in range(x_ref.shape[0])]
    for k, (x_ref, at) in enumerate(ks):
        c, d = divmod(k, lags)
        left_ref[c * points : (c + 1) * points, d * sensors : (d + 1) * sensors] = x_ref[at]


def adjoint_piece_body(start, slots, lags, *refs):
    group, (left_ref, out_ref, r_ref, all_ref) = refs[:-4], refs[-4:]
    points = out_ref.shape[1]
    for v, (_, total) in enumerate(adjoint_terms(group, start, left_ref, r_ref, all_ref, slots, lags, points)):
        out_ref[v] = total


def adjoint_last_body(near, slots, lags, n_groups, n_last, *refs):
    done, refs = refs[: near * n_groups - 1], refs[near * n_groups - 1 :]
    slots_ref, r_ref, all_ref = refs[-3:]
    vectors = slots_ref.shape[0]
    left_ref, groups, outs = refs[0], refs[1 : -3 - vectors], refs[-3 - vectors : -3]
    of_group, points, steps = done[0].shape
    of_block, lanes = of_group * n_groups, outs[0].shape[1]
    j = lax.axis_index("par")
    place, block = j // near, lax.rem(j, near)
    extra = 0.0
    for ref in groups:
        extra += ref[ref.shape[0] - EXTRA_ROWS :, :].astype(jnp.float32)
    squared = three_parts(jnp.full((1, lanes), jnp.sum(extra), jnp.float32))
    for i, ref in enumerate(done):
        away, group = i // n_groups, (place ^ (i % n_groups * slots)) // slots
        for v in range(of_group):
            slots_ref[(block ^ away) * of_block + group * of_group + v] = ref[v]
    start = (n_groups - 1) * slots
    for v, total in adjoint_terms(groups[-n_last:], start, left_ref, r_ref, all_ref, slots, lags, points):
        slots_ref[(block ^ (near - 1)) * of_block + v] = total
    for v, ref in enumerate(outs):
        for i in range(steps // lanes):
            some = slots_ref[v, :, i * lanes : (i + 1) * lanes]
            ref[i * points : (i + 1) * points, :] = some.astype(ref.dtype)
        ref[steps // lanes * points :, :] = squared.astype(ref.dtype)


def total_body(scale, *refs):
    terms, (gradient_ref, misfit_ref) = refs[:-2], refs[-2:]
    _, points, steps = gradient_ref.shape
    lanes = terms[0].shape[1]
    total = terms[0][...]
    for term in terms[1:]:
        total += term[...].astype(jnp.float32)
    for i in range(steps // lanes):
        gradient_ref[0, :, i * lanes : (i + 1) * lanes] = total[i * points : (i + 1) * points]
    at = steps // lanes * points
    misfit_ref[...] = jnp.sum(total[at:, :1], axis=0, keepdims=True) * scale


def call(body, out_shape, operands, limit=SMALL_LIMIT, **options):
    vmem = pl.BlockSpec(memory_space=pltpu.VMEM)
    options.setdefault("in_specs", [vmem] * len(operands))
    return pl.pallas_call(
        body,
        out_shape=out_shape,
        out_specs=jax.tree.map(lambda _: vmem, out_shape),
        compiler_params=pltpu.CompilerParams(vmem_limit_bytes=limit),
        **options,
    )(*operands)


def local(model, kernel, observed, weights):
    n_sens, n_par = lax.axis_size("sens"), lax.axis_size("par")
    sensors, points, steps = kernel.shape
    vectors = n_sens * model.shape[0]
    near, far = levels(n_par, vectors)
    of_block = vectors // near
    n_groups = 2 if of_block % 2 == 0 and far % 2 == 0 else 1
    slots = far // n_groups
    lags = 256 // points
    rows = vectors * steps // n_par
    lanes = min(128, steps)
    flops = 2 * vectors * sensors * points * steps * steps // near
    cost = pl.CostEstimate(flops=flops, bytes_accessed=2 * kernel.size, transcendentals=0)
    piece_cost = pl.CostEstimate(flops=flops // n_groups, bytes_accessed=2 * kernel.size, transcendentals=0)
    vmem, hbm = pl.BlockSpec(memory_space=pltpu.VMEM), pl.BlockSpec(memory_space=pltpu.HBM)

    def struct(shape, dtype):
        return jax.ShapeDtypeStruct(shape, dtype)

    models = [model] + [swap(model, "sens", step) for step in range(1, n_sens)]
    half = steps - steps // lanes // 2 * lanes
    xs = [jnp.transpose(kernel[:, :, :half], (2, 1, 0))]
    if half < steps:
        xs.append(
            call(
                turn_body,
                struct((steps - half, points, sensors), kernel.dtype),
                (kernel,),
                VMEM_LIMIT,
                scratch_shapes=[pltpu.VMEM(((steps - half) * points, sensors), jnp.float32)]
                + [pltpu.VMEM((sensors * points, lanes), jnp.float32)] * ((steps - half) // lanes),
                cost_estimate=pl.CostEstimate(flops=0, bytes_accessed=3 * kernel.size, transcendentals=0),
            )
        )

    def forward(away, start, count):
        of_part = of_block * count // far
        scratch = [
            pltpu.VMEM((vectors, points, steps), jnp.float32),
            pltpu.VMEM((of_part, lags * points, steps), jnp.float32),
            pltpu.VMEM((of_part, steps, lags * points), jnp.bfloat16),
            pltpu.VMEM((of_part * steps, sensors), jnp.float32),
        ]
        operands = [*models, *xs]
        specs = [vmem] * len(operands)
        if away == 0:
            scratch += [
                pltpu.VMEM((sensors, steps), jnp.float32),
                pltpu.VMEM((1, sensors), jnp.float32),
                pltpu.SemaphoreType.DMA((2,)),
            ]
            operands += [observed, weights[None, :]]
            specs += [hbm] * 2
            out = struct((count * rows + WEIGHT_ROWS, sensors), jnp.float32)
        else:
            out = struct((count * rows, sensors), jnp.bfloat16)
        return call(
            functools.partial(forward_body, away, start, count, near, lags, len(models), len(xs)),
            out,
            operands,
            VMEM_LIMIT,
            in_specs=specs,
            scratch_shapes=scratch,
            cost_estimate=cost if away == 0 else piece_cost,
        )

    crossed = [
        [swap(forward(away, g * slots, slots), "par", away) for away in range(1, near)]
        for g in range(n_groups - 1, -1, -1)
    ]
    sums = forward(0, 0, far)
    terms = []
    for g, some in zip(range(n_groups - 1, -1, -1), crossed):
        outs = [struct((rows, sensors), jnp.bfloat16)] * slots
        if g == 0:
            outs[0] = struct((rows + WEIGHT_ROWS, sensors), jnp.float32)
        outs = call(functools.partial(middle_body, near, g * slots, slots), outs, (sums, *some))
        if g == 0:
            own, *outs = outs
        first = far - len(terms) - 1
        terms += [swap(out, "par", b * near) for b, out in zip(range(first, 0, -1), outs[::-1])]
    residual = call(residual_body, struct((rows + EXTRA_ROWS, sensors), jnp.bfloat16), (own, *terms))
    parts = [residual] + [swap(residual, "par", b * near) for b in range(far - 1, 0, -1)][::-1]
    n_last = 2 if slots % 2 == 0 else 1
    starts = [*range(0, far - slots, slots), *range(far - slots, far, slots // n_last), far]
    pieces = []
    for start, end in zip(starts, starts[1:]):
        joined = struct(((end - start) * rows + EXTRA_ROWS, sensors), jnp.bfloat16)
        pieces.append(parts[start] if end - start == 1 else call(join_body, joined, parts[start:end]))
    groups = [[piece] for piece in pieces[:-n_last]] + [pieces[-n_last:]]

    of_group = of_block // n_groups
    scratch = [
        pltpu.VMEM((of_group, lags * sensors, steps), jnp.bfloat16),
        pltpu.VMEM((of_group * steps, sensors), jnp.float32),
    ]
    least_cost = pl.CostEstimate(flops=0, bytes_accessed=0, transcendentals=0)
    left = call(
        functools.partial(left_body, lags),
        struct((steps // lags * points, lags * sensors), jnp.bfloat16),
        xs,
        VMEM_LIMIT,
        cost_estimate=least_cost,
    )

    def adjoint_piece(i, group):
        return call(
            functools.partial(adjoint_piece_body, i % n_groups * slots, slots, lags),
            struct((of_group, points, steps), jnp.float32),
            (*group, left),
            VMEM_LIMIT,
            scratch_shapes=scratch,
            cost_estimate=least_cost if i < n_groups - 1 else cost,
        )

    done = [adjoint_piece(g, groups[g]) for g in range(n_groups - 1)]
    others = [[[swap(piece, "par", away) for piece in group] for group in groups] for away in range(1, near)]
    every = groups + [group for some in others for group in some]
    done += [adjoint_piece(i, every[i]) for i in range(len(done), len(every) - 1)]
    partials = call(
        functools.partial(adjoint_last_body, near, slots, lags, n_groups, n_last),
        [struct((steps // lanes * points + EXTRA_ROWS, lanes), jnp.bfloat16 if v else jnp.float32) for v in range(vectors)],
        (*done, left, *[piece for group in every for piece in group]),
        VMEM_LIMIT,
        scratch_shapes=[pltpu.VMEM((vectors, points, steps), jnp.float32)] + scratch,
        cost_estimate=piece_cost,
    )
    received = [swap(partials[step], "sens", step) for step in range(n_sens - 1, 0, -1)]
    entries = vectors * sensors * n_sens * steps
    gradient, misfit = call(
        functools.partial(total_body, 0.5 / entries),
        [struct((1, points, steps), jnp.float32), struct((1, 1), jnp.float32)],
        (partials[0], *received),
    )
    return (gradient, misfit[0, 0])


def solution(mesh):
    return jax.shard_map(
        local,
        mesh=mesh,
        in_specs=(P("sens", "par", None), P("sens", "par", None), P(None, "sens", None), P("sens")),
        out_specs=(P("sens", "par", None), P()),
        check_vma=False,
    )
```
